512 devices in a mesh: freq: 16 (over z, y_lo), brick: 32 (over y_hi, x, core).
Axes of the slice: x: 4, y: 8 (y_hi: 4, y_lo: 2; y = y_hi * 2 + y_lo), z: 8, core: 2. Of those that a mesh axis runs over, the one named last changes fastest.
Arguments:
- panels: bfloat16 [16, 2, 1024, 24576], P('freq', None, 'brick'), may hold values from -6 to 6
- freq_weight: float32 [16], P('freq'), may hold values from 0.5 to 2
- surface_weight: float32 [4096], replicated, may hold values from 0.25 to 4
- picks: int32 [1024], replicated, may hold values from 0 to 4095, as said below
- neighbours: int32 [192, 13], P('brick'), may hold values from -1 to 191, as said below
Outputs:
- hessian: bfloat16 [192, 13, 128, 128], P('brick', None, 'freq')
The draws below stay inside these ranges and needn't reach their ends.
Inputs may be any that keep to these rules, and one draw needn't show every extreme that they name: `picks`: strictly rising; the s-th entry lies in [s * 4, (s + 1) * 4). `neighbours`: bricks form a grid of 32 x 2 x 3 with id x * 2 * 3 + y * 3 + z. Row b lists, in an arbitrary order, the ids of the 13 bricks at offsets (1, dy, dz) for dy, dz in -1, 0, 1, (0, 1, dz) for dz in -1, 0, 1, and (0, 0, 1) from brick b, with -1 for an offset outside the grid.
All inputs are finite; a program needn't handle non-finite values.
Results may differ from the reference program's by a relative error of at most 0.022.
Values may be sent and summed in bfloat16 or wider, within the bound.
No kernel may reach another device: no remote copies, remote signals or barrier semaphores. Data moves between devices by JAX's collectives and lax.ppermute only.
A program may use at most 128 MiB of HBM per device.

```python
import math
import jax
import jax.numpy as jnp
import numpy as np
from jax import lax

CELLS = 128
S = 1024
S_ALL = 4096
NEIGH = 13
BRICK_Y = 2
BRICK_Z = 3
FREQ_DEV = 1
FREQ = 16
BRICKS = 192
N_FREQ = 16
N_BRICK = 32


forward_offsets = np.array([[1, -1, -1], [1, -1, 0], [1, -1, 1], [1, 0, -1], [1, 0, 0], [1, 0, 1], [1, 1, -1], [1, 1, 0], [1, 1, 1], [0, 1, -1], [0, 1, 0], [0, 1, 1], [0, 0, 1]], dtype=np.int32)


def draw_picks(key, part):
    key = jax.random.fold_in(key, 1)
    stride_len = S_ALL // S
    jitter = jax.random.randint(key, (S,), 0, stride_len)
    jitter = jitter.at[0].set(0).at[S - 1].set(stride_len - 1)
    return (jnp.arange(S, dtype=jnp.int32) * stride_len + jitter).astype(jnp.int32)


def draw_neighbours(key, part):
    key = jax.random.fold_in(key, 2)
    brick_keys = jax.random.split(key, BRICKS)
    slot_orders = jax.vmap(lambda brick_key: jax.random.permutation(brick_key, 13))(brick_keys)
    offsets = jnp.asarray(forward_offsets)[slot_orders]
    brick_ids = jnp.arange(BRICKS, dtype=jnp.int32)
    per_slab = BRICK_Y * BRICK_Z
    grid_x = brick_ids // per_slab
    grid_y = brick_ids // BRICK_Z % BRICK_Y
    grid_z = brick_ids % BRICK_Z
    near_x = grid_x[:, None] + offsets[:, :, 0]
    near_y = grid_y[:, None] + offsets[:, :, 1]
    near_z = grid_z[:, None] + offsets[:, :, 2]
    inside = (near_x < N_BRICK) & (near_y >= 0) & (near_y < BRICK_Y) & (near_z >= 0) & (near_z < BRICK_Z)
    ident = near_x * per_slab + near_y * BRICK_Z + near_z
    return jnp.where(inside, ident, -1).astype(jnp.int32)


def levels(key, extent, cuts, least, top_value):
    level, own = 1.0, jax.random.fold_in(key, 6)
    for axis_at, blocks in cuts:
        heights = jnp.exp(jax.random.uniform(jax.random.fold_in(own, axis_at), (blocks,), jnp.float32, least / len(cuts), top_value / len(cuts)))
        level = level * jnp.repeat(heights, extent[axis_at] // blocks).reshape([-1 if axis == axis_at else 1 for axis in range(len(extent))])
    return level


def noise(key, dims, spread, bound, cuts=(), kind=jnp.bfloat16):
    entries = spread * jax.random.normal(key, dims, jnp.float32)
    if cuts:
        entries = entries * levels(key, dims, cuts, -0.22, 0.18)
    return jnp.clip(entries, -bound, bound).astype(kind)


def setup_inputs(seed: int = 0) -> dict:
    streams_of = jax.random.split(jax.random.key(seed), 6)
    panels = noise(streams_of[0], (FREQ, 2, S, BRICKS * CELLS), 1.0, 6.0, ((0, 16), (2, 32)))
    freq_weight = jnp.clip(jnp.exp(math.log(2.0) - 1.3862944 * jax.random.uniform(streams_of[1], (FREQ,), jnp.float32) ** levels(streams_of[1], (FREQ,), ((0, 16),), -0.2, 0.2)), 0.5, 2.0)
    surface_weight = jnp.clip(jnp.exp(jax.random.uniform(streams_of[2], (S_ALL,), jnp.float32, math.log(0.25), math.log(4.0))), 0.25, 4.0)
    picks = draw_picks(jax.random.fold_in(streams_of[5], 71), 0)
    neighbours = draw_neighbours(jax.random.fold_in(streams_of[5], 71), 0)
    return dict(panels=panels, freq_weight=freq_weight, surface_weight=surface_weight, picks=picks, neighbours=neighbours)


def reference(panels, freq_weight, surface_weight, picks, neighbours):
    per_slab = BRICK_Y * BRICK_Z
    slab_width = per_slab * CELLS
    group_rows = FREQ_DEV * 2 * S
    factor = 1.0 / math.sqrt(2 * S * FREQ)
    weighting = freq_weight[:, None] * surface_weight[picks][None, :] * factor

    def slab(slab_index):
        own_panels = lax.dynamic_slice_in_dim(panels, slab_index * slab_width, slab_width, 3)
        next_start = jnp.minimum(slab_index + 1, N_BRICK - 1).astype(jnp.int32) * slab_width
        next_panels = lax.dynamic_slice_in_dim(panels, next_start, slab_width, 3)
        next_panels = jnp.where(slab_index + 1 < N_BRICK, next_panels, jnp.zeros_like(next_panels))
        weighted = (own_panels.astype(jnp.float32) * weighting[:, None, :, None]).astype(jnp.bfloat16)
        weighted = weighted.reshape(N_FREQ, group_rows, slab_width).astype(jnp.float32)
        candidates = jnp.concatenate([own_panels, next_panels], axis=3).reshape(N_FREQ, group_rows, 2 * slab_width).astype(jnp.float32)
        products = jnp.einsum('gra,grc->gac', weighted, candidates, precision=lax.Precision.HIGHEST)
        rounded = lax.optimization_barrier(products.astype(jnp.bfloat16))
        summed = lax.optimization_barrier(jnp.sum(rounded.astype(jnp.float32), axis=0))
        pair_blocks = summed.reshape(per_slab, CELLS, 2 * per_slab, CELLS).transpose(0, 2, 1, 3)
        listed = lax.dynamic_slice_in_dim(neighbours, slab_index * per_slab, per_slab, 0)
        present = listed >= 0
        relative = jnp.where(present, listed - slab_index * per_slab, 0).astype(jnp.int32)
        chosen = pair_blocks[jnp.arange(per_slab, dtype=jnp.int32)[:, None], relative]
        return jnp.where(present[:, :, None, None], chosen, jnp.zeros_like(chosen))
    every_slab = lax.map(slab, jnp.arange(N_BRICK, dtype=jnp.int32))
    return every_slab.reshape(BRICKS, NEIGH, CELLS, CELLS).astype(jnp.bfloat16)
```

```python
import math

import jax
import jax.numpy as jnp
import numpy as np
from jax import lax
from jax.experimental import pallas as pl
from jax.experimental.pallas import tpu as pltpu
from jax.sharding import Mesh
from jax.sharding import PartitionSpec as P

CELLS = 128
BRICK_Y = 2
BRICK_Z = 3
SLAB = BRICK_Y * BRICK_Z
WIDTH = SLAB * CELLS
AXES = ("zh", "zl", "yl", "yh", "x", "core")
SIZES = (4, 2, 2, 4, 4, 2)
GATHER = ("yl", "zl", "x")
REDUCE = ("zh", "yh")

NEXT_PAIRS = [
    ((y * 3 + z, 6 + first), (y * 3 + z, 7 + first))
    for z, firsts in ((0, (0, 3)), (1, (0, 2, 4)), (2, (1, 4)))
    for y in range(BRICK_Y)
    for first in firsts
]
OWN_PAIRS = [
    ((0, 3), (0, 4)),
    ((1, 4), (1, 5)),
    ((2, 4), (2, 5)),
    ((0, 1), (1, 2)),
    ((1, 3), (3, 4)),
    ((4, 5), None),
]
PAIRS = NEXT_PAIRS + OWN_PAIRS
ROWS = 16 * len(PAIRS)
SHARES = 16


def block_table():
    table = np.full((SLAB, 2 * SLAB), 2 * len(PAIRS), np.int32)
    for at, pair in enumerate(PAIRS):
        for half, block in enumerate(pair):
            if block is not None:
                table[block] = 2 * at + half
    return table


def pack_kernel(scale_ref, own_ref, next_ref, out_ref):
    scale = scale_ref[...]
    width = own_ref.shape[1]
    out_ref[0, :, :width] = (own_ref[...].astype(jnp.float32) * scale).astype(jnp.bfloat16)
    out_ref[0, :, width:] = (next_ref[...].astype(jnp.float32) * scale).astype(jnp.bfloat16)


def pack(panels, scale):
    rows, cells = panels.shape
    pairs = cells // (2 * WIDTH)
    return pl.pallas_call(
        pack_kernel,
        grid=(pairs,),
        in_specs=[
            pl.BlockSpec((rows, 1), lambda c: (0, 0)),
            pl.BlockSpec((rows, 2 * WIDTH), lambda c: (0, c)),
            pl.BlockSpec((rows, WIDTH), lambda c: (0, (2 * c + 2) % (2 * pairs))),
        ],
        out_specs=pl.BlockSpec((1, rows, 3 * WIDTH), lambda c: (c, 0, 0)),
        out_shape=jax.ShapeDtypeStruct((pairs, rows, 3 * WIDTH), jnp.bfloat16),
        name="pack",
    )(scale, panels, panels)


def blocks_kernel(slab_ref, own_ref, next_ref, out_ref, turned):
    del slab_ref
    for brick in range(SLAB):
        turned[brick * CELLS : (brick + 1) * CELLS, :] = own_ref[:, brick * CELLS : (brick + 1) * CELLS].T

    def candidates(first, count):
        ref, first = (own_ref, first) if first < SLAB else (next_ref, first - SLAB)
        return ref[:, first * CELLS : (first + count) * CELLS]

    def product(bricks, first, count):
        left = jnp.concatenate([turned[b * CELLS : (b + 1) * CELLS, :] for b in bricks], axis=0)
        made = jnp.dot(left, candidates(first, count), preferred_element_type=jnp.float32)
        return {
            (b, first + n): made[m * CELLS : (m + 1) * CELLS, n * CELLS : (n + 1) * CELLS]
            for m, b in enumerate(bricks)
            for n in range(count)
        }

    def store(at, pair, made):
        parts = [
            made[b].reshape(SHARES, CELLS // SHARES, CELLS) if b is not None
            else jnp.zeros((SHARES, CELLS // SHARES, CELLS), jnp.float32)
            for b in pair
        ]
        out_ref[:, 16 * at : 16 * (at + 1), :] = jnp.concatenate(parts, axis=1).astype(jnp.bfloat16)

    for z, firsts in ((0, (0, 3)), (1, (0, 2, 4)), (2, (1, 4))):
        bricks = (z, 3 + z)
        for first in firsts:
            made = product(bricks, SLAB + first, 2)
            for at, pair in enumerate(PAIRS):
                if pair[0] in made:
                    store(at, pair, made)
    made = product((0, 1, 2), 3, 3)
    made.update({k: v for k, v in product((0, 1), 1, 2).items() if k in ((0, 1), (1, 2))})
    made.update({k: v for k, v in product((3, 4), 4, 2).items() if k in ((3, 4), (4, 5))})
    for at in range(len(NEXT_PAIRS), len(PAIRS)):
        store(at, PAIRS[at], made)


def blocks(gathered, slab):
    rows = gathered.shape[0]
    return pl.pallas_call(
        blocks_kernel,
        grid_spec=pltpu.PrefetchScalarGridSpec(
            num_scalar_prefetch=1,
            grid=(1,),
            in_specs=[
                pl.BlockSpec((rows, WIDTH), lambda i, s: (0, s[0])),
                pl.BlockSpec((rows, WIDTH), lambda i, s: (0, s[0] + 1)),
            ],
            out_specs=pl.BlockSpec((SHARES, ROWS, CELLS), lambda i, s: (0, 0, 0)),
            scratch_shapes=[pltpu.VMEM((WIDTH, rows), jnp.bfloat16)],
        ),
        out_shape=jax.ShapeDtypeStruct((SHARES, ROWS, CELLS), jnp.bfloat16),
        compiler_params=pltpu.CompilerParams(vmem_limit_bytes=40 * 1024 * 1024),
        cost_estimate=pl.CostEstimate(
            flops=2 * 48 * CELLS * CELLS * rows, bytes_accessed=2 * rows * 2 * WIDTH + 2 * SHARES * ROWS * CELLS, transcendentals=0
        ),
        name="blocks",
    )(slab, gathered, gathered)


def slots_kernel(index_ref, held_ref, out_ref):
    for b in range(out_ref.shape[0]):
        for k in range(out_ref.shape[1]):
            at = index_ref[b, k]
            out_ref[b, k] = held_ref[at]


def slots(held, index):
    share = held.shape[1]
    return pl.pallas_call(
        slots_kernel,
        in_specs=[pl.BlockSpec(memory_space=pltpu.SMEM), pl.BlockSpec(memory_space=pltpu.VMEM)],
        out_specs=pl.BlockSpec(memory_space=pltpu.VMEM),
        out_shape=jax.ShapeDtypeStruct((*index.shape, share, CELLS), jnp.bfloat16),
        name="slots",
    )(index, held)


def owner_route():
    route = []
    for source in range(math.prod(SIZES)):
        zh, zl, yl, yh, x, core = (int(v) for v in np.unravel_index(source, SIZES))
        target = np.ravel_multi_index((zh, yh // 2, yh % 2, yl * 2 + zl, x, core), SIZES)
        route.append((source, int(target)))
    return route


def row_scale(freq_weight, surface_weight, picks, total_rows):
    points = picks.shape[0]
    stride = surface_weight.shape[0] // points
    devices = lax.axis_size(("yh", "x", "core"))
    own = points // devices
    first = lax.axis_index(("yh", "x", "core")) * own
    own_picks = lax.dynamic_slice_in_dim(picks, first, own, 0)
    own_surface = lax.dynamic_slice_in_dim(surface_weight, first * stride, own * stride, 0).reshape(own, stride)
    offset = own_picks - (first + jnp.arange(own, dtype=jnp.int32)) * stride
    hit = offset[:, None] == jnp.arange(stride, dtype=jnp.int32)[None, :]
    picked = jnp.sum(jnp.where(hit, own_surface, 0.0), axis=1)
    return jnp.sqrt(freq_weight[0] * picked * (1.0 / math.sqrt(total_rows)))


def shards(panels, freq_weight, surface_weight, picks, neighbours):
    freq_count, parts, own_points, cells = panels.shape
    points = picks.shape[0]
    total_rows = parts * points * lax.axis_size(("zh", "zl", "yl"))
    scale = row_scale(freq_weight, surface_weight, picks, total_rows)
    scale = jnp.tile(scale, parts)[:, None]
    rows = parts * own_points
    packed = pack(panels.reshape(rows, cells), scale)
    gathered = lax.all_to_all(packed, GATHER, split_axis=0, concat_axis=0, tiled=True)
    gathered = gathered.reshape(-1, 3 * WIDTH)
    core = lax.axis_index("core")
    other = blocks(gathered, (1 - core).reshape(1))
    arrived = lax.ppermute(other, "core", [(0, 1), (1, 0)])
    own = blocks(gathered, core.reshape(1))
    partial = (own.astype(jnp.float32) + arrived.astype(jnp.float32)).astype(jnp.bfloat16)
    spread = lax.all_to_all(partial, REDUCE, split_axis=0, concat_axis=0, tiled=True)
    held = jnp.sum(spread.astype(jnp.float32), axis=0).astype(jnp.bfloat16)
    held = lax.ppermute(held, AXES, owner_route())
    slab = lax.axis_index(("yh", "x", "core"))
    relative = neighbours - slab * SLAB
    at = relative[:, :, None] == jnp.arange(2 * SLAB, dtype=jnp.int32)[None, None, :]
    at = at & (neighbours >= 0)[:, :, None]
    nothing = 2 * len(PAIRS)
    index = nothing + jnp.sum(jnp.where(at, jnp.asarray(block_table() - nothing)[:, None, :], 0), axis=2)
    share = CELLS // SHARES
    held = jnp.concatenate([held, jnp.zeros((share, CELLS), jnp.bfloat16)], axis=0)
    return slots(held.reshape(-1, share, CELLS), index.astype(jnp.int32))


def solution(mesh):
    fine = Mesh(mesh.devices.reshape(SIZES), AXES)
    freq, brick = ("zh", "zl", "yl"), ("yh", "x", "core")
    in_specs = (P(freq, None, brick, None), P(freq), P(), P(), P(brick, None))
    out_specs = P(brick, None, freq, None)
    return jax.shard_map(shards, mesh=fine, in_specs=in_specs, out_specs=out_specs, check_vma=False)
```

```python
import functools
import math

import jax
import jax.numpy as jnp
import numpy as np
from jax import lax
from jax.experimental import pallas as pl
from jax.experimental.pallas import tpu as pltpu
from jax.sharding import Mesh
from jax.sharding import PartitionSpec as P

CELLS = 128
BRICK_Y = 2
BRICK_Z = 3
SLAB = BRICK_Y * BRICK_Z
WIDTH = SLAB * CELLS
AXES = ("zh", "zl", "yl", "yh", "x", "core")
SIZES = (4, 2, 2, 4, 4, 2)
GATHER = ("yl", "zl", "x")
REDUCE = ("zh", "yh")

NEXT_PAIRS = [
    ((y * 3 + z, 6 + first), (y * 3 + z, 7 + first))
    for z, firsts in ((0, (0, 3)), (1, (0, 2, 4)), (2, (1, 4)))
    for y in range(BRICK_Y)
    for first in firsts
]
OWN_PAIRS = [
    ((0, 3), (0, 4)),
    ((1, 4), (1, 5)),
    ((2, 4), (2, 5)),
    ((0, 1), (1, 2)),
    ((1, 3), (3, 4)),
    ((4, 5), None),
]
PAIRS = NEXT_PAIRS + OWN_PAIRS
ROWS = 16 * len(PAIRS)
SHARES = 16


def block_table():
    table = np.full((SLAB, 2 * SLAB), -1, np.int32)
    for at, pair in enumerate(PAIRS):
        for half, block in enumerate(pair):
            if block is not None:
                table[block] = 2 * at + half
    return table


def pack_kernel(freq_ref, surface_ref, picks_ref, own_ref, next_ref, out_ref, scale_ref, *, total_rows):
    @pl.when(pl.program_id(0) == 0)
    def _():
        rows = scale_ref.shape[0]
        own_points = rows // 2
        first = lax.axis_index(("yh", "x", "core")) * own_points
        row = lax.broadcasted_iota(jnp.int32, (own_points, CELLS), 0)
        picked = jnp.zeros((own_points, CELLS), jnp.float32)
        for point in range(own_points):
            picked = jnp.where(row == point, surface_ref[picks_ref[first + point]], picked)
        scale = jnp.sqrt(picked * (freq_ref[0] * (1.0 / math.sqrt(total_rows))))
        scale_ref[:own_points] = scale
        scale_ref[own_points:] = scale

    scale = scale_ref[:, :1]
    for pair in range(out_ref.shape[0]):
        first = pair * 2 * WIDTH
        if first + 3 * WIDTH <= own_ref.shape[1]:
            out_ref[pair] = (own_ref[:, first : first + 3 * WIDTH].astype(jnp.float32) * scale).astype(jnp.bfloat16)
        else:
            out_ref[pair, :, : 2 * WIDTH] = (own_ref[:, first:].astype(jnp.float32) * scale).astype(jnp.bfloat16)
            out_ref[pair, :, 2 * WIDTH :] = (next_ref[...].astype(jnp.float32) * scale).astype(jnp.bfloat16)


def pack(panels, freq_weight, surface_weight, picks, total_rows):
    rows, cells = panels.shape
    pairs = cells // (2 * WIDTH)
    step = 4
    return pl.pallas_call(
        functools.partial(pack_kernel, total_rows=total_rows),
        grid=(pairs // step,),
        in_specs=[
            pl.BlockSpec(memory_space=pltpu.SMEM),
            pl.BlockSpec(memory_space=pltpu.SMEM),
            pl.BlockSpec(memory_space=pltpu.SMEM),
            pl.BlockSpec((rows, 2 * WIDTH * step), lambda c: (0, c)),
            pl.BlockSpec((rows, WIDTH), lambda c: (0, (2 * step * (c + 1)) % (2 * pairs))),
        ],
        out_specs=pl.BlockSpec((step, rows, 3 * WIDTH), lambda c: (c, 0, 0)),
        out_shape=jax.ShapeDtypeStruct((pairs, rows, 3 * WIDTH), jnp.bfloat16),
        scratch_shapes=[pltpu.VMEM((rows, CELLS), jnp.float32)],
        compiler_params=pltpu.CompilerParams(vmem_limit_bytes=24 * 1024 * 1024),
        name="pack",
    )(freq_weight, surface_weight, picks, panels, panels)


def blocks_kernel(slab_ref, own_ref, next_ref, out_ref, turned):
    del slab_ref
    for brick in range(SLAB):
        turned[brick * CELLS : (brick + 1) * CELLS, :] = own_ref[:, brick * CELLS : (brick + 1) * CELLS].T

    def candidates(first, count):
        ref, first = (own_ref, first) if first < SLAB else (next_ref, first - SLAB)
        return ref[:, first * CELLS : (first + count) * CELLS]

    def product(bricks, first, count):
        left = jnp.concatenate([turned[b * CELLS : (b + 1) * CELLS, :] for b in bricks], axis=0)
        made = jnp.dot(left, candidates(first, count), preferred_element_type=jnp.float32)
        return {
            (b, first + n): made[m * CELLS : (m + 1) * CELLS, n * CELLS : (n + 1) * CELLS]
            for m, b in enumerate(bricks)
            for n in range(count)
        }

    def store(at, pair, made):
        parts = [
            made[b].reshape(SHARES, CELLS // SHARES, CELLS) if b is not None
            else jnp.zeros((SHARES, CELLS // SHARES, CELLS), jnp.float32)
            for b in pair
        ]
        out_ref[:, 16 * at : 16 * (at + 1), :] = jnp.concatenate(parts, axis=1).astype(jnp.bfloat16)

    for z, firsts in ((0, (0, 3)), (1, (0, 2, 4)), (2, (1, 4))):
        bricks = (z, 3 + z)
        for first in firsts:
            made = product(bricks, SLAB + first, 2)
            for at, pair in enumerate(PAIRS):
                if pair[0] in made:
                    store(at, pair, made)
    made = product((0, 1, 2), 3, 3)
    made.update({k: v for k, v in product((0, 1), 1, 2).items() if k in ((0, 1), (1, 2))})
    made.update({k: v for k, v in product((3, 4), 4, 2).items() if k in ((3, 4), (4, 5))})
    for at in range(len(NEXT_PAIRS), len(PAIRS)):
        store(at, PAIRS[at], made)


def blocks(gathered, slab):
    rows = gathered.shape[0]
    return pl.pallas_call(
        blocks_kernel,
        grid_spec=pltpu.PrefetchScalarGridSpec(
            num_scalar_prefetch=1,
            grid=(1,),
            in_specs=[
                pl.BlockSpec((rows, WIDTH), lambda i, s: (0, s[0])),
                pl.BlockSpec((rows, WIDTH), lambda i, s: (0, s[0] + 1)),
            ],
            out_specs=pl.BlockSpec((SHARES, ROWS, CELLS), lambda i, s: (0, 0, 0)),
            scratch_shapes=[pltpu.VMEM((WIDTH, rows), jnp.bfloat16)],
        ),
        out_shape=jax.ShapeDtypeStruct((SHARES, ROWS, CELLS), jnp.bfloat16),
        compiler_params=pltpu.CompilerParams(vmem_limit_bytes=24 * 1024 * 1024),
        cost_estimate=pl.CostEstimate(
            flops=2 * 48 * CELLS * CELLS * rows, bytes_accessed=2 * rows * 2 * WIDTH + 2 * SHARES * ROWS * CELLS, transcendentals=0
        ),
        name="blocks",
    )(slab, gathered, gathered)


def slots_kernel(index_ref, held_ref, out_ref):
    for b in range(out_ref.shape[0]):
        for k in range(out_ref.shape[1]):
            at = index_ref[b, k]
            block = held_ref[jnp.maximum(at, 0)]
            out_ref[b, k] = jnp.where(at >= 0, block, jnp.zeros_like(block))


def slots(held, index):
    share = held.shape[1]
    return pl.pallas_call(
        slots_kernel,
        in_specs=[pl.BlockSpec(memory_space=pltpu.SMEM), pl.BlockSpec(memory_space=pltpu.VMEM)],
        out_specs=pl.BlockSpec(memory_space=pltpu.VMEM),
        out_shape=jax.ShapeDtypeStruct((*index.shape, share, CELLS), jnp.bfloat16),
        compiler_params=pltpu.CompilerParams(vmem_limit_bytes=16 * 1024 * 1024),
        name="slots",
    )(index, held)


def owner_route():
    route = []
    for source in range(math.prod(SIZES)):
        zh, zl, yl, yh, x, core = (int(v) for v in np.unravel_index(source, SIZES))
        target = np.ravel_multi_index((zh, yh // 2, yh % 2, yl * 2 + zl, x, core), SIZES)
        route.append((source, int(target)))
    return route


def shards(panels, freq_weight, surface_weight, picks, neighbours):
    freq_count, parts, own_points, cells = panels.shape
    points = picks.shape[0]
    total_rows = parts * points * lax.axis_size(("zh", "zl", "yl"))
    rows = parts * own_points
    packed = pack(panels.reshape(rows, cells), freq_weight, surface_weight, picks, total_rows)
    gathered = lax.all_to_all(packed, GATHER, split_axis=0, concat_axis=0, tiled=True)
    gathered = gathered.reshape(-1, 3 * WIDTH)
    core = lax.axis_index("core")
    other = blocks(gathered, (1 - core).reshape(1))
    arrived = lax.ppermute(other, "core", [(0, 1), (1, 0)])
    own = blocks(gathered, core.reshape(1))
    partial = (own.astype(jnp.float32) + arrived.astype(jnp.float32)).astype(jnp.bfloat16)
    spread = lax.all_to_all(partial, REDUCE, split_axis=0, concat_axis=0, tiled=True)
    held = jnp.sum(spread.astype(jnp.float32), axis=0).astype(jnp.bfloat16)
    held = lax.ppermute(held, AXES, owner_route())
    slab = lax.axis_index(("yh", "x", "core"))
    relative = neighbours - slab * SLAB
    at = relative[:, :, None] == jnp.arange(2 * SLAB, dtype=jnp.int32)[None, None, :]
    at = at & (neighbours >= 0)[:, :, None]
    index = jnp.sum(jnp.where(at, jnp.asarray(block_table() + 1)[:, None, :], 0), axis=2) - 1
    share = CELLS // SHARES
    return slots(held.reshape(-1, share, CELLS), index.astype(jnp.int32))


def solution(mesh):
    fine = Mesh(mesh.devices.reshape(SIZES), AXES)
    freq, brick = ("zh", "zl", "yl"), ("yh", "x", "core")
    in_specs = (P(freq, None, brick, None), P(freq), P(), P(), P(brick, None))
    out_specs = P(brick, None, freq, None)
    return jax.shard_map(shards, mesh=fine, in_specs=in_specs, out_specs=out_specs, check_vma=False)
```

```python
import functools
import math

import jax
import jax.numpy as jnp
import numpy as np
from jax import lax
from jax.experimental import pallas as pl
from jax.experimental.pallas import tpu as pltpu
from jax.sharding import Mesh
from jax.sharding import PartitionSpec as P

CELLS = 128
BRICK_Y = 2
BRICK_Z = 3
SLAB = BRICK_Y * BRICK_Z
WIDTH = SLAB * CELLS
AXES = ("zh", "zl", "yl", "yh", "x", "core")
SIZES = (4, 2, 2, 4, 4, 2)
GATHER = ("yl", "zl", "x")
REDUCE = ("zh", "yh")

NEXT_PAIRS = [
    ((y * 3 + z, 6 + first), (y * 3 + z, 7 + first))
    for z, firsts in ((0, (0, 3)), (1, (0, 2, 4)), (2, (1, 4)))
    for y in range(BRICK_Y)
    for first in firsts
]
OWN_PAIRS = [
    ((0, 3), (0, 4)),
    ((1, 4), (1, 5)),
    ((2, 4), (2, 5)),
    ((0, 1), (1, 2)),
    ((1, 3), (3, 4)),
    ((4, 5), None),
]
PAIRS = NEXT_PAIRS + OWN_PAIRS
ROWS = 16 * len(PAIRS)
SHARES = 16


def block_table():
    table = np.full((SLAB, 2 * SLAB), -1, np.int32)
    for at, pair in enumerate(PAIRS):
        for half, block in enumerate(pair):
            if block is not None:
                table[block] = 2 * at + half
    return table


def pack_kernel(freq_ref, surface_ref, picks_ref, panels_ref, out_ref, held, made, arrived, left, *, total_rows):
    rows, cells = held.shape
    pairs = made.shape[0]
    chunks = arrived.shape[0]
    width = cells // chunks

    def fetch(chunk):
        columns = pl.ds(chunk * width, width)
        return pltpu.make_async_copy(panels_ref.at[:, columns], held.at[:, columns], arrived.at[chunk])

    def store(pair):
        return pltpu.make_async_copy(made.at[pair], out_ref.at[pair], left.at[pair])

    for chunk in range(chunks):
        fetch(chunk).start()
    own_points = rows // 2
    first = lax.axis_index(("yh", "x", "core")) * own_points
    row = lax.broadcasted_iota(jnp.int32, (own_points, CELLS), 0)
    picked = jnp.zeros((own_points, CELLS), jnp.float32)
    for point in range(own_points):
        picked = jnp.where(row == point, surface_ref[picks_ref[first + point]], picked)
    scale = jnp.sqrt(picked * (freq_ref[0] * (1.0 / math.sqrt(total_rows))))
    scale = jnp.concatenate([scale, scale], axis=0)
    scale = jnp.concatenate([scale] * SLAB, axis=1)
    slabs = 2 * pairs
    for slab in range(slabs):
        if slab * chunks % slabs == 0:
            fetch(slab * chunks // slabs).wait()
        block = (held[:, slab * WIDTH : (slab + 1) * WIDTH].astype(jnp.float32) * scale).astype(jnp.bfloat16)
        made[slab // 2, :, slab % 2 * WIDTH : (slab % 2 + 1) * WIDTH] = block
        if slab % 2 == 0:
            made[(slab // 2 - 1) % pairs, :, 2 * WIDTH :] = block
            if slab > 0:
                store(slab // 2 - 1).start()
    store(pairs - 1).start()
    for pair in range(pairs):
        store(pair).wait()


def pack(panels, freq_weight, surface_weight, picks, total_rows):
    rows, cells = panels.shape
    pairs = cells // (2 * WIDTH)
    return pl.pallas_call(
        functools.partial(pack_kernel, total_rows=total_rows),
        in_specs=[
            pl.BlockSpec(memory_space=pltpu.SMEM),
            pl.BlockSpec(memory_space=pltpu.SMEM),
            pl.BlockSpec(memory_space=pltpu.SMEM),
            pl.BlockSpec(memory_space=pl.ANY),
        ],
        out_specs=pl.BlockSpec(memory_space=pl.ANY),
        out_shape=jax.ShapeDtypeStruct((pairs, rows, 3 * WIDTH), jnp.bfloat16),
        scratch_shapes=[
            pltpu.VMEM((rows, cells), jnp.bfloat16),
            pltpu.VMEM((pairs, rows, 3 * WIDTH), jnp.bfloat16),
            pltpu.SemaphoreType.DMA((8,)),
            pltpu.SemaphoreType.DMA((pairs,)),
        ],
        compiler_params=pltpu.CompilerParams(vmem_limit_bytes=54 * 1024 * 1024),
        name="pack",
    )(freq_weight, surface_weight, picks, panels)


def blocks_kernel(gathered_ref, out_ref, turned, *, own):
    core = lax.axis_index("core")
    start = (core if own else 1 - core) * WIDTH

    def columns(first, count):
        return gathered_ref[:, pl.ds(pl.multiple_of(start + first * CELLS, CELLS), count * CELLS)]

    for brick in range(SLAB):
        turned[brick * CELLS : (brick + 1) * CELLS, :] = columns(brick, 1).T

    def product(bricks, first, count):
        left = jnp.concatenate([turned[b * CELLS : (b + 1) * CELLS, :] for b in bricks], axis=0)
        made = jnp.dot(left, columns(first, count), preferred_element_type=jnp.float32)
        return {
            (b, first + n): made[m * CELLS : (m + 1) * CELLS, n * CELLS : (n + 1) * CELLS]
            for m, b in enumerate(bricks)
            for n in range(count)
        }

    def store(at, pair, made):
        parts = [
            made[b].reshape(SHARES, CELLS // SHARES, CELLS) if b is not None
            else jnp.zeros((SHARES, CELLS // SHARES, CELLS), jnp.float32)
            for b in pair
        ]
        out_ref[:, 16 * at : 16 * (at + 1), :] = jnp.concatenate(parts, axis=1).astype(jnp.bfloat16)

    for z, firsts in ((0, (0, 3)), (1, (0, 2, 4)), (2, (1, 4))):
        bricks = (z, 3 + z)
        for first in firsts:
            made = product(bricks, SLAB + first, 2)
            for at, pair in enumerate(PAIRS):
                if pair[0] in made:
                    store(at, pair, made)
    made = product((0, 1, 2), 3, 3)
    made.update({k: v for k, v in product((0, 1), 1, 2).items() if k in ((0, 1), (1, 2))})
    made.update({k: v for k, v in product((3, 4), 4, 2).items() if k in ((3, 4), (4, 5))})
    for at in range(len(NEXT_PAIRS), len(PAIRS)):
        store(at, PAIRS[at], made)


def blocks(gathered, own):
    rows = gathered.shape[0]
    return pl.pallas_call(
        functools.partial(blocks_kernel, own=own),
        in_specs=[pl.BlockSpec(memory_space=pltpu.VMEM)],
        out_specs=pl.BlockSpec(memory_space=pltpu.VMEM),
        out_shape=jax.ShapeDtypeStruct((SHARES, ROWS, CELLS), jnp.bfloat16),
        scratch_shapes=[pltpu.VMEM((WIDTH, rows), jnp.bfloat16)],
        compiler_params=pltpu.CompilerParams(vmem_limit_bytes=24 * 1024 * 1024),
        cost_estimate=pl.CostEstimate(
            flops=2 * 48 * CELLS * CELLS * rows, bytes_accessed=2 * rows * 2 * WIDTH + 2 * SHARES * ROWS * CELLS, transcendentals=0
        ),
        name="blocks",
    )(gathered)


def slots_kernel(index_ref, held_ref, out_ref):
    for b in range(out_ref.shape[0]):
        for k in range(out_ref.shape[1]):
            at = index_ref[b, k]
            block = held_ref[jnp.maximum(at, 0)]
            out_ref[b, k] = jnp.where(at >= 0, block, jnp.zeros_like(block))


def slots(held, index):
    share = held.shape[1]
    return pl.pallas_call(
        slots_kernel,
        in_specs=[pl.BlockSpec(memory_space=pltpu.SMEM), pl.BlockSpec(memory_space=pltpu.VMEM)],
        out_specs=pl.BlockSpec(memory_space=pltpu.VMEM),
        out_shape=jax.ShapeDtypeStruct((*index.shape, share, CELLS), jnp.bfloat16),
        compiler_params=pltpu.CompilerParams(vmem_limit_bytes=16 * 1024 * 1024),
        name="slots",
    )(index, held)


def owner_route():
    route = []
    for source in range(math.prod(SIZES)):
        zh, zl, yl, yh, x, core = (int(v) for v in np.unravel_index(source, SIZES))
        target = np.ravel_multi_index((zh, yh // 2, yh % 2, yl * 2 + zl, x, core), SIZES)
        route.append((source, int(target)))
    return route


def block_index(neighbours):
    slab = lax.axis_index(("yh", "x", "core"))
    relative = neighbours - slab * SLAB
    at = relative[:, :, None] == jnp.arange(2 * SLAB, dtype=jnp.int32)[None, None, :]
    at = at & (neighbours >= 0)[:, :, None]
    return jnp.sum(jnp.where(at, jnp.asarray(block_table() + 1)[:, None, :], 0), axis=2).astype(jnp.int32) - 1


def shards(panels, freq_weight, surface_weight, picks, neighbours):
    freq_count, parts, own_points, cells = panels.shape
    points = picks.shape[0]
    total_rows = parts * points * lax.axis_size(("zh", "zl", "yl"))
    rows = parts * own_points
    packed = pack(panels.reshape(rows, cells), freq_weight, surface_weight, picks, total_rows)
    gathered = lax.all_to_all(packed, GATHER, split_axis=0, concat_axis=0, tiled=True)
    gathered = gathered.reshape(-1, 3 * WIDTH)
    other = blocks(gathered, False)
    neighbours, other = lax.optimization_barrier((neighbours, other))
    arrived = lax.ppermute(other, "core", [(0, 1), (1, 0)])
    index = block_index(neighbours)
    own = blocks(gathered, True)
    partial = (own.astype(jnp.float32) + arrived.astype(jnp.float32)).astype(jnp.bfloat16)
    partial, index = lax.optimization_barrier((partial, index))
    spread = lax.all_to_all(partial, REDUCE, split_axis=0, concat_axis=0, tiled=True)
    held = jnp.sum(spread.astype(jnp.float32), axis=0).astype(jnp.bfloat16)
    held = lax.ppermute(held, AXES, owner_route())
    return slots(held.reshape(-1, CELLS // SHARES, CELLS), index)


def solution(mesh):
    fine = Mesh(mesh.devices.reshape(SIZES), AXES)
    freq, brick = ("zh", "zl", "yl"), ("yh", "x", "core")
    in_specs = (P(freq, None, brick, None), P(freq), P(), P(), P(brick, None))
    out_specs = P(brick, None, freq, None)
    return jax.shard_map(shards, mesh=fine, in_specs=in_specs, out_specs=out_specs, check_vma=False)
```

```python
import functools
import math

import jax
import jax.numpy as jnp
import numpy as np
from jax import lax
from jax.experimental import pallas as pl
from jax.experimental.pallas import tpu as pltpu
from jax.sharding import Mesh
from jax.sharding import PartitionSpec as P

CELLS = 128
BRICK_Y = 2
BRICK_Z = 3
SLAB = BRICK_Y * BRICK_Z
WIDTH = SLAB * CELLS
AXES = ("zh", "zl", "yl", "yh", "x", "core")
SIZES = (4, 2, 2, 4, 4, 2)
GATHER = ("yl", "zl", "x")

NEXT_PAIRS = [
    ((y * 3 + z, 6 + first), (y * 3 + z, 7 + first))
    for z, firsts in ((0, (0, 3)), (1, (0, 2, 4)), (2, (1, 4)))
    for y in range(BRICK_Y)
    for first in firsts
]
OWN_PAIRS = [
    ((0, 3), (0, 4)),
    ((1, 4), (1, 5)),
    ((2, 4), (2, 5)),
    ((0, 1), (1, 2)),
    ((1, 3), (3, 4)),
    ((4, 5), None),
]
PAIRS = NEXT_PAIRS + OWN_PAIRS
ROWS = 16 * len(PAIRS)
SHARES = 16


def block_table():
    table = np.full((SLAB, 2 * SLAB), -1, np.int32)
    for at, pair in enumerate(PAIRS):
        for half, block in enumerate(pair):
            if block is not None:
                table[block] = 2 * at + half
    return table


def pack_kernel(freq_ref, surface_ref, picks_ref, panels_ref, out_ref, held, made, arrived, left, *, total_rows):
    rows, cells = held.shape
    pairs = made.shape[0]
    chunks = arrived.shape[0]
    width = cells // chunks

    def fetch(chunk):
        columns = pl.ds(chunk * width, width)
        return pltpu.make_async_copy(panels_ref.at[:, columns], held.at[:, columns], arrived.at[chunk])

    def store(pair):
        return pltpu.make_async_copy(made.at[pair], out_ref.at[pair], left.at[pair])

    for chunk in range(chunks):
        fetch(chunk).start()
    own_points = rows // 2
    first = lax.axis_index(("yh", "x", "core")) * own_points
    row = lax.broadcasted_iota(jnp.int32, (own_points, CELLS), 0)
    picked = jnp.zeros((own_points, CELLS), jnp.float32)
    for point in range(own_points):
        picked = jnp.where(row == point, surface_ref[picks_ref[first + point]], picked)
    scale = jnp.sqrt(picked * (freq_ref[0] * (1.0 / math.sqrt(total_rows))))
    scale = jnp.concatenate([scale, scale], axis=0)
    scale = jnp.concatenate([scale] * SLAB, axis=1)
    slabs = 2 * pairs
    for slab in range(slabs):
        if slab * chunks % slabs == 0:
            fetch(slab * chunks // slabs).wait()
        block = (held[:, slab * WIDTH : (slab + 1) * WIDTH].astype(jnp.float32) * scale).astype(jnp.bfloat16)
        made[slab // 2, :, slab % 2 * WIDTH : (slab % 2 + 1) * WIDTH] = block
        if slab % 2 == 0:
            made[(slab // 2 - 1) % pairs, :, 2 * WIDTH :] = block
            if slab > 0:
                store(slab // 2 - 1).start()
    store(pairs - 1).start()
    for pair in range(pairs):
        store(pair).wait()


def pack(panels, freq_weight, surface_weight, picks, total_rows):
    rows, cells = panels.shape
    pairs = cells // (2 * WIDTH)
    return pl.pallas_call(
        functools.partial(pack_kernel, total_rows=total_rows),
        in_specs=[
            pl.BlockSpec(memory_space=pltpu.SMEM),
            pl.BlockSpec(memory_space=pltpu.SMEM),
            pl.BlockSpec(memory_space=pltpu.SMEM),
            pl.BlockSpec(memory_space=pl.ANY),
        ],
        out_specs=pl.BlockSpec(memory_space=pl.ANY),
        out_shape=jax.ShapeDtypeStruct((pairs, rows, 3 * WIDTH), jnp.bfloat16),
        scratch_shapes=[
            pltpu.VMEM((rows, cells), jnp.bfloat16),
            pltpu.VMEM((pairs, rows, 3 * WIDTH), jnp.bfloat16),
            pltpu.SemaphoreType.DMA((8,)),
            pltpu.SemaphoreType.DMA((pairs,)),
        ],
        compiler_params=pltpu.CompilerParams(vmem_limit_bytes=54 * 1024 * 1024),
        name="pack",
    )(freq_weight, surface_weight, picks, panels)


def blocks_kernel(gathered_ref, out_ref, turned, *, own):
    core = lax.axis_index("core")
    start = (core if own else 1 - core) * WIDTH

    def columns(first, count):
        return gathered_ref[:, pl.ds(pl.multiple_of(start + first * CELLS, CELLS), count * CELLS)]

    for brick in range(SLAB):
        turned[brick * CELLS : (brick + 1) * CELLS, :] = columns(brick, 1).T

    def product(bricks, first, count):
        left = jnp.concatenate([turned[b * CELLS : (b + 1) * CELLS, :] for b in bricks], axis=0)
        made = jnp.dot(left, columns(first, count), preferred_element_type=jnp.float32)
        return {
            (b, first + n): made[m * CELLS : (m + 1) * CELLS, n * CELLS : (n + 1) * CELLS]
            for m, b in enumerate(bricks)
            for n in range(count)
        }

    def store(at, pair, made):
        parts = [
            made[b].reshape(SHARES, CELLS // SHARES, CELLS) if b is not None
            else jnp.zeros((SHARES, CELLS // SHARES, CELLS), jnp.float32)
            for b in pair
        ]
        out_ref[:, 16 * at : 16 * (at + 1), :] = jnp.concatenate(parts, axis=1).astype(jnp.bfloat16)

    for z, firsts in ((0, (0, 3)), (1, (0, 2, 4)), (2, (1, 4))):
        bricks = (z, 3 + z)
        for first in firsts:
            made = product(bricks, SLAB + first, 2)
            for at, pair in enumerate(PAIRS):
                if pair[0] in made:
                    store(at, pair, made)
    made = product((0, 1, 2), 3, 3)
    made.update({k: v for k, v in product((0, 1), 1, 2).items() if k in ((0, 1), (1, 2))})
    made.update({k: v for k, v in product((3, 4), 4, 2).items() if k in ((3, 4), (4, 5))})
    for at in range(len(NEXT_PAIRS), len(PAIRS)):
        store(at, PAIRS[at], made)


def blocks(gathered, own):
    rows = gathered.shape[0]
    return pl.pallas_call(
        functools.partial(blocks_kernel, own=own),
        in_specs=[pl.BlockSpec(memory_space=pltpu.VMEM)],
        out_specs=pl.BlockSpec(memory_space=pltpu.VMEM),
        out_shape=jax.ShapeDtypeStruct((SHARES, ROWS, CELLS), jnp.bfloat16),
        scratch_shapes=[pltpu.VMEM((WIDTH, rows), jnp.bfloat16)],
        compiler_params=pltpu.CompilerParams(vmem_limit_bytes=12 * 1024 * 1024),
        cost_estimate=pl.CostEstimate(
            flops=2 * 48 * CELLS * CELLS * rows, bytes_accessed=2 * rows * 2 * WIDTH + 2 * SHARES * ROWS * CELLS, transcendentals=0
        ),
        name="blocks",
    )(gathered)


def slots_kernel(index_ref, held_ref, out_ref):
    for b in range(out_ref.shape[0]):
        for k in range(out_ref.shape[1]):
            at = index_ref[b, k]
            block = held_ref[jnp.maximum(at, 0)]
            out_ref[b, k] = jnp.where(at >= 0, block, jnp.zeros_like(block))


def slots(held, index):
    share = held.shape[1]
    return pl.pallas_call(
        slots_kernel,
        in_specs=[pl.BlockSpec(memory_space=pltpu.SMEM), pl.BlockSpec(memory_space=pltpu.VMEM)],
        out_specs=pl.BlockSpec(memory_space=pltpu.VMEM),
        out_shape=jax.ShapeDtypeStruct((*index.shape, share, CELLS), jnp.bfloat16),
        compiler_params=pltpu.CompilerParams(vmem_limit_bytes=16 * 1024 * 1024),
        name="slots",
    )(index, held)


def places():
    for device in range(math.prod(SIZES)):
        yield device, dict(zip(AXES, (int(v) for v in np.unravel_index(device, SIZES))))


def split_axes(core):
    return ("yh", "zh") if core == 0 else ("zh", "yh")


def split_groups(step):
    groups = {}
    for device, at in places():
        axis = split_axes(at["core"])[step]
        groups.setdefault(tuple(v for a, v in at.items() if a != axis), []).append(device)
    return list(groups.values())


def owner_route():
    route = []
    for source, at in places():
        first, second = split_axes(at["core"])
        share = at[first] * 4 + at[second]
        owner = (share // 4, share // 2 % 2, share % 2, at["yl"] * 2 + at["zl"], at["x"], at["core"])
        route.append((source, int(np.ravel_multi_index(owner, SIZES))))
    return route


def summed_over(partial, step):
    groups = split_groups(step)
    parts = len(groups[0])
    shape = partial.shape
    partial = partial.reshape(parts, shape[0] // parts * shape[1], shape[2])
    spread = lax.all_to_all(partial, AXES, split_axis=0, concat_axis=0, tiled=True, axis_index_groups=groups)
    summed = jnp.sum(spread.astype(jnp.float32), axis=0).astype(jnp.bfloat16)
    return summed.reshape(shape[0] // parts, *shape[1:])


def block_index(neighbours):
    slab = lax.axis_index(("yh", "x", "core"))
    relative = neighbours - slab * SLAB
    at = relative[:, :, None] == jnp.arange(2 * SLAB, dtype=jnp.int32)[None, None, :]
    at = at & (neighbours >= 0)[:, :, None]
    return jnp.sum(jnp.where(at, jnp.asarray(block_table() + 1)[:, None, :], 0), axis=2).astype(jnp.int32) - 1


def shards(panels, freq_weight, surface_weight, picks, neighbours):
    freq_count, parts, own_points, cells = panels.shape
    points = picks.shape[0]
    total_rows = parts * points * lax.axis_size(("zh", "zl", "yl"))
    rows = parts * own_points
    packed = pack(panels.reshape(rows, cells), freq_weight, surface_weight, picks, total_rows)
    gathered = lax.all_to_all(packed, GATHER, split_axis=0, concat_axis=0, tiled=True)
    gathered = gathered.reshape(-1, 3 * WIDTH)
    other = blocks(gathered, False)
    neighbours, other = lax.optimization_barrier((neighbours, other))
    arrived = lax.ppermute(other, "core", [(0, 1), (1, 0)])
    index = block_index(neighbours)
    own = blocks(gathered, True)
    partial = (own.astype(jnp.float32) + arrived.astype(jnp.float32)).astype(jnp.bfloat16)
    partial, index = lax.optimization_barrier((partial, index))
    held = summed_over(summed_over(partial, 0), 1)
    held = lax.ppermute(held, AXES, owner_route())
    return slots(held.reshape(-1, CELLS // SHARES, CELLS), index)


def solution(mesh):
    fine = Mesh(mesh.devices.reshape(SIZES), AXES)
    freq, brick = ("zh", "zl", "yl"), ("yh", "x", "core")
    in_specs = (P(freq, None, brick, None), P(freq), P(), P(), P(brick, None))
    out_specs = P(brick, None, freq, None)
    return jax.shard_map(shards, mesh=fine, in_specs=in_specs, out_specs=out_specs, check_vma=False)
```

```python
import functools
import math

import jax
import jax.numpy as jnp
import numpy as np
from jax import lax
from jax.experimental import pallas as pl
from jax.experimental.pallas import tpu as pltpu
from jax.sharding import Mesh
from jax.sharding import PartitionSpec as P

CELLS = 128
BRICK_Y = 2
BRICK_Z = 3
SLAB = BRICK_Y * BRICK_Z
WIDTH = SLAB * CELLS
AXES = ("zh", "zl", "yl", "yh", "x", "core")
SIZES = (4, 2, 2, 4, 4, 2)

NEXT_PAIRS = [
    ((y * 3 + z, 6 + first), (y * 3 + z, 7 + first))
    for z, firsts in ((0, (0, 3)), (1, (0, 2, 4)), (2, (1, 4)))
    for y in range(BRICK_Y)
    for first in firsts
]
OWN_PAIRS = [
    ((0, 3), (0, 4)),
    ((1, 4), (1, 5)),
    ((2, 4), (2, 5)),
    ((0, 1), (1, 2)),
    ((1, 3), (3, 4)),
    ((4, 5), None),
]
PAIRS = NEXT_PAIRS + OWN_PAIRS
ROWS = 16 * len(PAIRS)
SPLIT = 4
SHARES = SPLIT * SPLIT
OWNED = 2
SET = 2 * OWNED


def block_table():
    table = np.full((SLAB, 2 * SLAB), -1, np.int32)
    for at, pair in enumerate(PAIRS):
        for half, block in enumerate(pair):
            if block is not None:
                table[block] = 2 * at + half
    return table


def pack_kernel(freq_ref, surface_ref, picks_ref, panels_ref, out_ref, held, made, arrived, left, *, total_rows):
    rows, cells = held.shape
    sets = made.shape[0]
    chunks = arrived.shape[0]
    width = cells // chunks

    def fetch(chunk):
        columns = pl.ds(chunk * width, width)
        return pltpu.make_async_copy(panels_ref.at[:, columns], held.at[:, columns], arrived.at[chunk])

    def store(at):
        return pltpu.make_async_copy(made.at[at], out_ref.at[at], left.at[at])

    for chunk in range(chunks):
        fetch(chunk).start()
    own_points = rows // 2
    first = lax.axis_index(("yh", "x", "core")) * own_points
    row = lax.broadcasted_iota(jnp.int32, (own_points, CELLS), 0)
    picked = jnp.zeros((own_points, CELLS), jnp.float32)
    for point in range(own_points):
        picked = jnp.where(row == point, surface_ref[picks_ref[first + point]], picked)
    scale = jnp.sqrt(picked * (freq_ref[0] * (1.0 / math.sqrt(total_rows))))
    scale = jnp.concatenate([scale, scale], axis=0)
    scale = jnp.concatenate([scale] * SLAB, axis=1)
    slabs = SET * sets
    for slab in range(slabs):
        if slab * chunks % slabs == 0:
            fetch(slab * chunks // slabs).wait()
        block = (held[:, slab * WIDTH : (slab + 1) * WIDTH].astype(jnp.float32) * scale).astype(jnp.bfloat16)
        at, place = slab // SET, slab % SET
        made[at, :, place * WIDTH : (place + 1) * WIDTH] = block
        if place == 0:
            made[(at - 1) % sets, :, SET * WIDTH :] = block
            if at > 0:
                store(at - 1).start()
    store(sets - 1).start()
    for at in range(sets):
        store(at).wait()


def pack(panels, freq_weight, surface_weight, picks, total_rows):
    rows, cells = panels.shape
    sets = cells // (SET * WIDTH)
    return pl.pallas_call(
        functools.partial(pack_kernel, total_rows=total_rows),
        in_specs=[
            pl.BlockSpec(memory_space=pltpu.SMEM),
            pl.BlockSpec(memory_space=pltpu.SMEM),
            pl.BlockSpec(memory_space=pltpu.SMEM),
            pl.BlockSpec(memory_space=pl.ANY),
        ],
        out_specs=pl.BlockSpec(memory_space=pl.ANY),
        out_shape=jax.ShapeDtypeStruct((sets, rows, (SET + 1) * WIDTH), jnp.bfloat16),
        scratch_shapes=[
            pltpu.VMEM((rows, cells), jnp.bfloat16),
            pltpu.VMEM((sets, rows, (SET + 1) * WIDTH), jnp.bfloat16),
            pltpu.SemaphoreType.DMA((8,)),
            pltpu.SemaphoreType.DMA((sets,)),
        ],
        compiler_params=pltpu.CompilerParams(vmem_limit_bytes=54 * 1024 * 1024),
        name="pack",
    )(freq_weight, surface_weight, picks, panels)


def blocks_kernel(gathered_ref, out_ref, turned, *, own):
    core = lax.axis_index("core")
    holder = core if own else 1 - core
    for turn in range(OWNED):
        slab_blocks(gathered_ref, out_ref, turned, holder + OWNED * turn, turn)


def slab_blocks(gathered_ref, out_ref, turned, slab, turn):
    def columns(first, count):
        start = pl.multiple_of(slab * WIDTH + first * CELLS, CELLS)
        return gathered_ref[:, pl.ds(start, count * CELLS)]

    for brick in range(SLAB):
        turned[brick * CELLS : (brick + 1) * CELLS, :] = columns(brick, 1).T

    def product(bricks, first, count):
        left = jnp.concatenate([turned[b * CELLS : (b + 1) * CELLS, :] for b in bricks], axis=0)
        made = jnp.dot(left, columns(first, count), preferred_element_type=jnp.float32)
        return {
            (b, first + n): made[m * CELLS : (m + 1) * CELLS, n * CELLS : (n + 1) * CELLS]
            for m, b in enumerate(bricks)
            for n in range(count)
        }

    def store(at, pair, made):
        parts = [
            made[b].reshape(SHARES, CELLS // SHARES, CELLS) if b is not None
            else jnp.zeros((SHARES, CELLS // SHARES, CELLS), jnp.float32)
            for b in pair
        ]
        rows = jnp.concatenate(parts, axis=1).astype(jnp.bfloat16)
        out_ref[:, turn, :, 16 * at : 16 * (at + 1), :] = rows.reshape(SPLIT, SPLIT, 16, CELLS)

    for z, firsts in ((0, (0, 3)), (1, (0, 2, 4)), (2, (1, 4))):
        bricks = (z, 3 + z)
        for first in firsts:
            made = product(bricks, SLAB + first, 2)
            for at, pair in enumerate(PAIRS):
                if pair[0] in made:
                    store(at, pair, made)
    made = product((0, 1, 2), 3, 3)
    made.update({k: v for k, v in product((0, 1), 1, 2).items() if k in ((0, 1), (1, 2))})
    made.update({k: v for k, v in product((3, 4), 4, 2).items() if k in ((3, 4), (4, 5))})
    for at in range(len(NEXT_PAIRS), len(PAIRS)):
        store(at, PAIRS[at], made)


def blocks(gathered, own):
    rows = gathered.shape[0]
    return pl.pallas_call(
        functools.partial(blocks_kernel, own=own),
        in_specs=[pl.BlockSpec(memory_space=pltpu.VMEM)],
        out_specs=pl.BlockSpec(memory_space=pltpu.VMEM),
        out_shape=jax.ShapeDtypeStruct((SPLIT, OWNED, SPLIT, ROWS, CELLS), jnp.bfloat16),
        scratch_shapes=[pltpu.VMEM((WIDTH, rows), jnp.bfloat16)],
        compiler_params=pltpu.CompilerParams(vmem_limit_bytes=16 * 1024 * 1024),
        cost_estimate=pl.CostEstimate(
            flops=OWNED * 2 * 48 * CELLS * CELLS * rows,
            bytes_accessed=OWNED * (2 * rows * 2 * WIDTH + 2 * SHARES * ROWS * CELLS),
            transcendentals=0,
        ),
        name="blocks",
    )(gathered)


def slots_kernel(neighbours_ref, table_ref, held_ref, out_ref):
    first = lax.axis_index(("yh", "x", "core")) * SLAB
    for b in range(out_ref.shape[0]):
        for k in range(out_ref.shape[1]):
            neighbour = neighbours_ref[b, k]
            at = table_ref[b, jnp.clip(neighbour - first, 0, 2 * SLAB - 1)]
            block = held_ref[jnp.maximum(at, 0)]
            out_ref[b, k] = jnp.where((neighbour >= 0) & (at >= 0), block, jnp.zeros_like(block))


def slots(held, neighbours):
    share = held.shape[1]
    return pl.pallas_call(
        slots_kernel,
        in_specs=[
            pl.BlockSpec(memory_space=pltpu.SMEM),
            pl.BlockSpec(memory_space=pltpu.SMEM),
            pl.BlockSpec(memory_space=pltpu.VMEM),
        ],
        out_specs=pl.BlockSpec(memory_space=pltpu.VMEM),
        out_shape=jax.ShapeDtypeStruct((*neighbours.shape, share, CELLS), jnp.bfloat16),
        compiler_params=pltpu.CompilerParams(vmem_limit_bytes=16 * 1024 * 1024),
        name="slots",
    )(neighbours, jnp.asarray(block_table()), held)


def places():
    for device in range(math.prod(SIZES)):
        yield device, dict(zip(AXES, (int(v) for v in np.unravel_index(device, SIZES))))


def gather_groups():
    groups = {}
    for device, at in places():
        core = at["core"]
        y, z = at["yh"] * 2 + at["yl"], at["zh"] * 2 + at["zl"]
        pairs = ((at["x"] - core) % 4 // 2, (y - core) % 8 // 2, (z - core) % 8 // 2, core)
        groups.setdefault(pairs, []).append((at["yl"], at["zl"], at["x"] % 2, device))
    return [[member[-1] for member in sorted(group)] for group in groups.values()]


def split_axes(core):
    return ("yh", "zh") if core == 0 else ("zh", "yh")


def split_groups(step):
    groups = {}
    for device, at in places():
        half = at["x"] // 2
        first, second = split_axes(at["core"])
        if step == 0:
            rest, place = (at["zl"], at["yl"], at[second], at["x"] % 2, at["core"]), (at[first], half)
        else:
            rest, place = (at["zl"], at["yl"], at[first], at["x"], at["core"]), (at[second],)
        groups.setdefault(rest, []).append((place, device))
    return [[device for _, device in sorted(group)] for group in groups.values()]


def owner_route():
    route = []
    for source, at in places():
        first, second = split_axes(at["core"])
        share = at[first] * SPLIT + at[second]
        x = 2 * (at["x"] % 2) + at["x"] // 2
        owner = (share // 4, share // 2 % 2, share % 2, at["yl"] * 2 + at["zl"], x, at["core"])
        route.append((source, int(np.ravel_multi_index(owner, SIZES))))
    return route


def summed_over(partial, step):
    groups = split_groups(step)
    parts = len(groups[0])
    partial = partial.reshape(parts, -1, CELLS)
    spread = lax.all_to_all(partial, AXES, split_axis=0, concat_axis=0, tiled=True, axis_index_groups=groups)
    return jnp.sum(spread.astype(jnp.float32), axis=0).astype(jnp.bfloat16)


def shards(panels, freq_weight, surface_weight, picks, neighbours):
    freq_count, parts, own_points, cells = panels.shape
    points = picks.shape[0]
    total_rows = parts * points * lax.axis_size(("zh", "zl", "yl"))
    rows = parts * own_points
    packed = pack(panels.reshape(rows, cells), freq_weight, surface_weight, picks, total_rows)
    gathered = lax.all_to_all(packed, AXES, split_axis=0, concat_axis=0, tiled=True, axis_index_groups=gather_groups())
    gathered = gathered.reshape(-1, (SET + 1) * WIDTH)
    other = blocks(gathered, False)
    arrived = lax.ppermute(other, "core", [(0, 1), (1, 0)])
    own = blocks(gathered, True)
    partial = (own.astype(jnp.float32) + arrived.astype(jnp.float32)).astype(jnp.bfloat16)
    held = summed_over(summed_over(partial, 0), 1)
    held = lax.ppermute(held, AXES, owner_route())
    return slots(held.reshape(-1, CELLS // SHARES, CELLS), neighbours)


def solution(mesh):
    fine = Mesh(mesh.devices.reshape(SIZES), AXES)
    freq, brick = ("zh", "zl", "yl"), ("yh", "x", "core")
    in_specs = (P(freq, None, brick, None), P(freq), P(), P(), P(brick, None))
    out_specs = P(brick, None, freq, None)
    return jax.shard_map(shards, mesh=fine, in_specs=in_specs, out_specs=out_specs, check_vma=False)
```

```python
import functools
import math

import jax
import jax.numpy as jnp
import numpy as np
from jax import lax
from jax.experimental import pallas as pl
from jax.experimental.pallas import tpu as pltpu
from jax.sharding import Mesh
from jax.sharding import PartitionSpec as P

CELLS = 128
BRICK_Y = 2
BRICK_Z = 3
SLAB = BRICK_Y * BRICK_Z
WIDTH = SLAB * CELLS
AXES = ("zh", "zl", "yl", "yh", "x", "core")
SIZES = (4, 2, 2, 4, 4, 2)

NEXT_PAIRS = [
    ((y * 3 + z, 6 + first), (y * 3 + z, 7 + first))
    for z, firsts in ((0, (0, 3)), (1, (0, 2, 4)), (2, (1, 4)))
    for y in range(BRICK_Y)
    for first in firsts
]
OWN_PAIRS = [
    ((0, 3), (0, 4)),
    ((1, 4), (1, 5)),
    ((2, 4), (2, 5)),
    ((0, 1), (1, 2)),
    ((1, 3), (3, 4)),
    ((4, 5), None),
]
PAIRS = NEXT_PAIRS + OWN_PAIRS
ROWS = 16 * len(PAIRS)
SPLIT = 4
SHARES = SPLIT * SPLIT
OWNED = 2
SET = 2 * OWNED


def block_table():
    table = np.full((SLAB, 2 * SLAB), -1, np.int32)
    for at, pair in enumerate(PAIRS):
        for half, block in enumerate(pair):
            if block is not None:
                table[block] = 2 * at + half
    return table


def pack_kernel(freq_ref, surface_hbm, picks_hbm, panels_ref, out_ref, surface_ref, picks_ref, held, made, small, arrived, left, *, total_rows):
    rows, cells = held.shape
    sets = made.shape[0]
    chunks = arrived.shape[0]
    width = cells // chunks

    def fetch(chunk):
        columns = pl.ds(chunk * width, width)
        return pltpu.make_async_copy(panels_ref.at[:, columns], held.at[:, columns], arrived.at[chunk])

    def store(at):
        return pltpu.make_async_copy(made.at[at], out_ref.at[at], left.at[at])

    points = [
        pltpu.make_async_copy(surface_hbm, surface_ref, small.at[0]),
        pltpu.make_async_copy(picks_hbm, picks_ref, small.at[1]),
    ]
    for copy in points:
        copy.start()
    for chunk in range(chunks):
        fetch(chunk).start()
    for copy in points:
        copy.wait()
    own_points = rows // 2
    first = lax.axis_index(("yh", "x", "core")) * own_points
    row = lax.broadcasted_iota(jnp.int32, (own_points, CELLS), 0)
    picked = jnp.zeros((own_points, CELLS), jnp.float32)
    for point in range(own_points):
        picked = jnp.where(row == point, surface_ref[picks_ref[first + point]], picked)
    scale = jnp.sqrt(picked * (freq_ref[...] * (1.0 / math.sqrt(total_rows))))
    scale = jnp.concatenate([scale, scale], axis=0)
    scale = jnp.concatenate([scale] * SLAB, axis=1)
    slabs = SET * sets
    for slab in range(slabs):
        if slab * chunks % slabs == 0:
            fetch(slab * chunks // slabs).wait()
        block = (held[:, slab * WIDTH : (slab + 1) * WIDTH].astype(jnp.float32) * scale).astype(jnp.bfloat16)
        at, place = slab // SET, slab % SET
        made[at, :, place * WIDTH : (place + 1) * WIDTH] = block
        if place == 0:
            made[(at - 1) % sets, :, SET * WIDTH :] = block
            if at > 0:
                store(at - 1).start()
    store(sets - 1).start()
    for at in range(sets):
        store(at).wait()


def pack(panels, freq_weight, surface_weight, picks, total_rows):
    rows, cells = panels.shape
    sets = cells // (SET * WIDTH)
    return pl.pallas_call(
        functools.partial(pack_kernel, total_rows=total_rows),
        in_specs=[
            pl.BlockSpec(memory_space=pltpu.VMEM),
            pl.BlockSpec(memory_space=pl.ANY),
            pl.BlockSpec(memory_space=pl.ANY),
            pl.BlockSpec(memory_space=pl.ANY),
        ],
        out_specs=pl.BlockSpec(memory_space=pl.ANY),
        out_shape=jax.ShapeDtypeStruct((sets, rows, (SET + 1) * WIDTH), jnp.bfloat16),
        scratch_shapes=[
            pltpu.SMEM(surface_weight.shape, jnp.float32),
            pltpu.SMEM(picks.shape, jnp.int32),
            pltpu.VMEM((rows, cells), jnp.bfloat16),
            pltpu.VMEM((sets, rows, (SET + 1) * WIDTH), jnp.bfloat16),
            pltpu.SemaphoreType.DMA((2,)),
            pltpu.SemaphoreType.DMA((8,)),
            pltpu.SemaphoreType.DMA((sets,)),
        ],
        compiler_params=pltpu.CompilerParams(vmem_limit_bytes=54 * 1024 * 1024),
        name="pack",
    )(freq_weight.reshape(1, 1), surface_weight, picks, panels)


def blocks_kernel(gathered_ref, out_ref, turned, *, own):
    core = lax.axis_index("core")
    holder = core if own else 1 - core
    for turn in range(OWNED):
        slab_blocks(gathered_ref, out_ref, turned, holder, turn)


def slab_blocks(gathered_ref, out_ref, turned, holder, turn):
    slab = holder + OWNED * turn

    def columns(first, count):
        start = pl.multiple_of(slab * WIDTH + first * CELLS, CELLS)
        return gathered_ref[:, pl.ds(start, count * CELLS)]

    for brick in range(SLAB):
        turned[brick * CELLS : (brick + 1) * CELLS, :] = columns(brick, 1).T

    def product(bricks, first, count):
        left = jnp.concatenate([turned[b * CELLS : (b + 1) * CELLS, :] for b in bricks], axis=0)
        made = jnp.dot(left, columns(first, count), preferred_element_type=jnp.float32)
        return {
            (b, first + n): made[m * CELLS : (m + 1) * CELLS, n * CELLS : (n + 1) * CELLS]
            for m, b in enumerate(bricks)
            for n in range(count)
        }

    def store(at, pair, made):
        parts = [
            made[b].reshape(SHARES, CELLS // SHARES, CELLS) if b is not None
            else jnp.zeros((SHARES, CELLS // SHARES, CELLS), jnp.float32)
            for b in pair
        ]
        rows = jnp.concatenate(parts, axis=1).astype(jnp.bfloat16)
        for share in range(SHARES):
            along_z, along_y = share // SPLIT, share % SPLIT
            first = jnp.where(holder == 0, along_y, along_z)
            second = jnp.where(holder == 0, along_z, along_y)
            out_ref[first, turn, second, 16 * at : 16 * (at + 1), :] = rows[share]

    for z, firsts in ((0, (0, 3)), (1, (0, 2, 4)), (2, (1, 4))):
        bricks = (z, 3 + z)
        for first in firsts:
            made = product(bricks, SLAB + first, 2)
            for at, pair in enumerate(PAIRS):
                if pair[0] in made:
                    store(at, pair, made)
    made = product((0, 1, 2), 3, 3)
    made.update({k: v for k, v in product((0, 1), 1, 2).items() if k in ((0, 1), (1, 2))})
    made.update({k: v for k, v in product((3, 4), 4, 2).items() if k in ((3, 4), (4, 5))})
    for at in range(len(NEXT_PAIRS), len(PAIRS)):
        store(at, PAIRS[at], made)


def blocks(gathered, own):
    rows = gathered.shape[0]
    return pl.pallas_call(
        functools.partial(blocks_kernel, own=own),
        in_specs=[pl.BlockSpec(memory_space=pltpu.VMEM)],
        out_specs=pl.BlockSpec(memory_space=pltpu.VMEM),
        out_shape=jax.ShapeDtypeStruct((SPLIT, OWNED, SPLIT, ROWS, CELLS), jnp.bfloat16),
        scratch_shapes=[pltpu.VMEM((WIDTH, rows), jnp.bfloat16)],
        compiler_params=pltpu.CompilerParams(vmem_limit_bytes=16 * 1024 * 1024),
        cost_estimate=pl.CostEstimate(
            flops=OWNED * 2 * 48 * CELLS * CELLS * rows,
            bytes_accessed=OWNED * (2 * rows * 2 * WIDTH + 2 * SHARES * ROWS * CELLS),
            transcendentals=0,
        ),
        name="blocks",
    )(gathered)


def slots_kernel(neighbours_ref, table_ref, held_ref, out_ref):
    first = lax.axis_index(("yh", "x", "core")) * SLAB
    for b in range(out_ref.shape[0]):
        for k in range(out_ref.shape[1]):
            neighbour = neighbours_ref[b, k]
            at = table_ref[b, jnp.clip(neighbour - first, 0, 2 * SLAB - 1)]
            block = held_ref[jnp.maximum(at, 0)]
            out_ref[b, k] = jnp.where((neighbour >= 0) & (at >= 0), block, jnp.zeros_like(block))


def slots(held, neighbours):
    share = held.shape[1]
    return pl.pallas_call(
        slots_kernel,
        in_specs=[
            pl.BlockSpec(memory_space=pltpu.SMEM),
            pl.BlockSpec(memory_space=pltpu.SMEM),
            pl.BlockSpec(memory_space=pltpu.VMEM),
        ],
        out_specs=pl.BlockSpec(memory_space=pltpu.VMEM),
        out_shape=jax.ShapeDtypeStruct((*neighbours.shape, share, CELLS), jnp.bfloat16),
        compiler_params=pltpu.CompilerParams(vmem_limit_bytes=16 * 1024 * 1024),
        name="slots",
    )(neighbours, jnp.asarray(block_table()), held)


def places():
    for device in range(math.prod(SIZES)):
        yield device, dict(zip(AXES, (int(v) for v in np.unravel_index(device, SIZES))))


def gather_groups():
    groups = {}
    for device, at in places():
        core = at["core"]
        y, z = at["yh"] * 2 + at["yl"], at["zh"] * 2 + at["zl"]
        pairs = ((at["x"] - core) % 4 // 2, (y - core) % 8 // 2, (z - core) % 8 // 2, core)
        groups.setdefault(pairs, []).append((at["yl"], at["zl"], at["x"] % 2, device))
    return [[member[-1] for member in sorted(group)] for group in groups.values()]


def split_axes(core):
    return ("yh", "zh") if core == 0 else ("zh", "yh")


def split_groups(step):
    groups = {}
    for device, at in places():
        half = at["x"] // 2
        first, second = split_axes(at["core"])
        if step == 0:
            rest, place = (at["zl"], at["yl"], at[second], at["x"] % 2, at["core"]), (at[first], half)
        else:
            rest, place = (at["zl"], at["yl"], at[first], at["x"], at["core"]), (at[second],)
        groups.setdefault(rest, []).append((place, device))
    return [[device for _, device in sorted(group)] for group in groups.values()]


def owner_route():
    route = []
    for source, at in places():
        share = at["zh"] * SPLIT + at["yh"]
        x = 2 * (at["x"] % 2) + at["x"] // 2
        owner = (share // 4, share // 2 % 2, share % 2, at["yl"] * 2 + at["zl"], x, at["core"])
        route.append((source, int(np.ravel_multi_index(owner, SIZES))))
    return route


def summed_over(partial, step):
    groups = split_groups(step)
    parts = len(groups[0])
    partial = partial.reshape(parts, -1, CELLS)
    spread = lax.all_to_all(partial, AXES, split_axis=0, concat_axis=0, tiled=True, axis_index_groups=groups)
    return jnp.sum(spread.astype(jnp.float32), axis=0).astype(jnp.bfloat16)


def shards(panels, freq_weight, surface_weight, picks, neighbours):
    freq_count, parts, own_points, cells = panels.shape
    points = picks.shape[0]
    total_rows = parts * points * lax.axis_size(("zh", "zl", "yl"))
    rows = parts * own_points
    packed = pack(panels.reshape(rows, cells), freq_weight, surface_weight, picks, total_rows)
    gathered = lax.all_to_all(packed, AXES, split_axis=0, concat_axis=0, tiled=True, axis_index_groups=gather_groups())
    gathered = gathered.reshape(-1, (SET + 1) * WIDTH)
    other = blocks(gathered, False)
    arrived = lax.ppermute(other, "core", [(0, 1), (1, 0)])
    own = blocks(gathered, True)
    partial = (own.astype(jnp.float32) + arrived.astype(jnp.float32)).astype(jnp.bfloat16)
    held = summed_over(summed_over(partial, 0), 1)
    held = lax.ppermute(held, AXES, owner_route())
    return slots(held.reshape(-1, CELLS // SHARES, CELLS), neighbours)


def solution(mesh):
    fine = Mesh(mesh.devices.reshape(SIZES), AXES)
    freq, brick = ("zh", "zl", "yl"), ("yh", "x", "core")
    in_specs = (P(freq, None, brick, None), P(freq), P(), P(), P(brick, None))
    out_specs = P(brick, None, freq, None)
    return jax.shard_map(shards, mesh=fine, in_specs=in_specs, out_specs=out_specs, check_vma=False)
```

```python
import functools
import math

import jax
import jax.numpy as jnp
import numpy as np
from jax import lax
from jax.experimental import pallas as pl
from jax.experimental.pallas import tpu as pltpu
from jax.sharding import Mesh
from jax.sharding import PartitionSpec as P

CELLS = 128
BRICK_Y = 2
BRICK_Z = 3
SLAB = BRICK_Y * BRICK_Z
WIDTH = SLAB * CELLS
AXES = ("zh", "zl", "yl", "yh", "x", "core")
SIZES = (4, 2, 2, 4, 4, 2)

NEXT_PAIRS = [
    ((y * 3 + z, 6 + first), (y * 3 + z, 7 + first))
    for z, firsts in ((0, (0, 3)), (1, (0, 2, 4)), (2, (1, 4)))
    for y in range(BRICK_Y)
    for first in firsts
]
OWN_PAIRS = [
    ((0, 3), (0, 4)),
    ((1, 4), (1, 5)),
    ((2, 4), (2, 5)),
    ((0, 1), (1, 2)),
    ((1, 3), (3, 4)),
    ((4, 5), None),
]
PAIRS = NEXT_PAIRS + OWN_PAIRS
ROWS = 8 * sum(block is not None for pair in PAIRS for block in pair)
SPLIT = 4
SHARES = SPLIT * SPLIT
OWNED = 2
SET = 2 * OWNED


def block_table():
    table = np.full((SLAB, 2 * SLAB), -1, np.int32)
    for at, pair in enumerate(PAIRS):
        for half, block in enumerate(pair):
            if block is not None:
                table[block] = 2 * at + half
    return table


def pack_kernel(freq_hbm, surface_hbm, picks_hbm, panels_ref, out_ref, freq_ref, surface_ref, picks_ref, held, made, small, arrived, left, *, total_rows):
    rows, cells = held.shape
    sets = made.shape[0]
    chunks = arrived.shape[0]
    width = cells // chunks

    def fetch(chunk):
        columns = pl.ds(chunk * width, width)
        return pltpu.make_async_copy(panels_ref.at[:, columns], held.at[:, columns], arrived.at[chunk])

    def store(at):
        return pltpu.make_async_copy(made.at[at], out_ref.at[at], left.at[at])

    points = [
        pltpu.make_async_copy(surface_hbm, surface_ref, small.at[0]),
        pltpu.make_async_copy(picks_hbm, picks_ref, small.at[1]),
        pltpu.make_async_copy(freq_hbm, freq_ref, small.at[2]),
    ]
    for copy in points:
        copy.start()
    for chunk in range(chunks):
        fetch(chunk).start()
    for copy in points:
        copy.wait()
    own_points = rows // 2
    first = lax.axis_index(("yh", "x", "core")) * own_points
    row = lax.broadcasted_iota(jnp.int32, (own_points, CELLS), 0)
    picked = jnp.zeros((own_points, CELLS), jnp.float32)
    for point in range(own_points):
        picked = jnp.where(row == point, surface_ref[picks_ref[first + point]], picked)
    scale = jnp.sqrt(picked * (freq_ref[0] * (1.0 / math.sqrt(total_rows))))
    scale = jnp.concatenate([scale, scale], axis=0)
    scale = jnp.concatenate([scale] * SLAB, axis=1)
    slabs = SET * sets
    for slab in range(slabs):
        if slab * chunks % slabs == 0:
            fetch(slab * chunks // slabs).wait()
        block = (held[:, slab * WIDTH : (slab + 1) * WIDTH].astype(jnp.float32) * scale).astype(jnp.bfloat16)
        at, place = slab // SET, slab % SET
        made[at, :, place * WIDTH : (place + 1) * WIDTH] = block
        if place == 0:
            made[(at - 1) % sets, :, SET * WIDTH :] = block
            if at > 0:
                store(at - 1).start()
    store(sets - 1).start()
    for at in range(sets):
        store(at).wait()


def pack(panels, freq_weight, surface_weight, picks, total_rows):
    rows, cells = panels.shape
    sets = cells // (SET * WIDTH)
    return pl.pallas_call(
        functools.partial(pack_kernel, total_rows=total_rows),
        in_specs=[
            pl.BlockSpec(memory_space=pl.ANY),
            pl.BlockSpec(memory_space=pl.ANY),
            pl.BlockSpec(memory_space=pl.ANY),
            pl.BlockSpec(memory_space=pl.ANY),
        ],
        out_specs=pl.BlockSpec(memory_space=pl.ANY),
        out_shape=jax.ShapeDtypeStruct((sets, rows, (SET + 1) * WIDTH), jnp.bfloat16),
        scratch_shapes=[
            pltpu.SMEM(freq_weight.shape, jnp.float32),
            pltpu.SMEM(surface_weight.shape, jnp.float32),
            pltpu.SMEM(picks.shape, jnp.int32),
            pltpu.VMEM((rows, cells), jnp.bfloat16),
            pltpu.VMEM((sets, rows, (SET + 1) * WIDTH), jnp.bfloat16),
            pltpu.SemaphoreType.DMA((3,)),
            pltpu.SemaphoreType.DMA((8,)),
            pltpu.SemaphoreType.DMA((sets,)),
        ],
        compiler_params=pltpu.CompilerParams(vmem_limit_bytes=54 * 1024 * 1024),
        name="pack",
    )(freq_weight, surface_weight, picks, panels)


def blocks_kernel(gathered_ref, out_ref, turned, *, own):
    core = lax.axis_index("core")
    holder = core if own else 1 - core
    for turn in range(OWNED):
        slab_blocks(gathered_ref, out_ref, turned, holder, turn)


def slab_blocks(gathered_ref, out_ref, turned, holder, turn):
    slab = holder + OWNED * turn

    def columns(first, count):
        start = pl.multiple_of(slab * WIDTH + first * CELLS, CELLS)
        return gathered_ref[:, pl.ds(start, count * CELLS)]

    for brick in range(SLAB):
        turned[brick * CELLS : (brick + 1) * CELLS, :] = columns(brick, 1).T

    def product(bricks, first, count):
        left = jnp.concatenate([turned[b * CELLS : (b + 1) * CELLS, :] for b in bricks], axis=0)
        made = jnp.dot(left, columns(first, count), preferred_element_type=jnp.float32)
        return {
            (b, first + n): made[m * CELLS : (m + 1) * CELLS, n * CELLS : (n + 1) * CELLS]
            for m, b in enumerate(bricks)
            for n in range(count)
        }

    def store(at, pair, made):
        parts = [made[b].reshape(SHARES, CELLS // SHARES, CELLS) for b in pair if b is not None]
        rows = jnp.concatenate(parts, axis=1).astype(jnp.bfloat16)
        for share in range(SHARES):
            along_z, along_y = share // SPLIT, share % SPLIT
            first = jnp.where(holder == 0, along_z, along_y)
            second = jnp.where(holder == 0, along_y, along_z)
            out_ref[first, turn, second, 16 * at : 16 * at + rows.shape[1], :] = rows[share]

    for z, firsts in ((0, (0, 3)), (1, (0, 2, 4)), (2, (1, 4))):
        bricks = (z, 3 + z)
        for first in firsts:
            made = product(bricks, SLAB + first, 2)
            for at, pair in enumerate(PAIRS):
                if pair[0] in made:
                    store(at, pair, made)
    made = product((0, 1, 2), 3, 3)
    made.update({k: v for k, v in product((0, 1), 1, 2).items() if k in ((0, 1), (1, 2))})
    made.update({k: v for k, v in product((3, 4), 4, 2).items() if k in ((3, 4), (4, 5))})
    for at in range(len(NEXT_PAIRS), len(PAIRS)):
        store(at, PAIRS[at], made)


def blocks(gathered, own):
    rows = gathered.shape[0]
    return pl.pallas_call(
        functools.partial(blocks_kernel, own=own),
        in_specs=[pl.BlockSpec(memory_space=pltpu.VMEM)],
        out_specs=pl.BlockSpec(memory_space=pltpu.VMEM),
        out_shape=jax.ShapeDtypeStruct((SPLIT, OWNED, SPLIT, ROWS, CELLS), jnp.bfloat16),
        scratch_shapes=[pltpu.VMEM((WIDTH, rows), jnp.bfloat16)],
        compiler_params=pltpu.CompilerParams(vmem_limit_bytes=16 * 1024 * 1024),
        cost_estimate=pl.CostEstimate(
            flops=OWNED * 2 * 48 * CELLS * CELLS * rows,
            bytes_accessed=OWNED * (2 * rows * 2 * WIDTH + 2 * SHARES * ROWS * CELLS),
            transcendentals=0,
        ),
        name="blocks",
    )(gathered)


def slots_kernel(neighbours_ref, table_ref, held_ref, out_ref):
    first = lax.axis_index(("yh", "x", "core")) * SLAB
    for b in range(out_ref.shape[0]):
        for k in range(out_ref.shape[1]):
            neighbour = neighbours_ref[b, k]
            at = table_ref[b, jnp.clip(neighbour - first, 0, 2 * SLAB - 1)]
            block = held_ref[jnp.maximum(at, 0)]
            out_ref[b, k] = jnp.where((neighbour >= 0) & (at >= 0), block, jnp.zeros_like(block))


def slots(held, neighbours):
    share = held.shape[1]
    return pl.pallas_call(
        slots_kernel,
        in_specs=[
            pl.BlockSpec(memory_space=pltpu.SMEM),
            pl.BlockSpec(memory_space=pltpu.SMEM),
            pl.BlockSpec(memory_space=pltpu.VMEM),
        ],
        out_specs=pl.BlockSpec(memory_space=pltpu.VMEM),
        out_shape=jax.ShapeDtypeStruct((*neighbours.shape, share, CELLS), jnp.bfloat16),
        compiler_params=pltpu.CompilerParams(vmem_limit_bytes=16 * 1024 * 1024),
        name="slots",
    )(neighbours, jnp.asarray(block_table()), held)


def places():
    for device in range(math.prod(SIZES)):
        yield device, dict(zip(AXES, (int(v) for v in np.unravel_index(device, SIZES))))


def gather_groups():
    groups = {}
    for device, at in places():
        core = at["core"]
        y, z = at["yh"] * 2 + at["yl"], at["zh"] * 2 + at["zl"]
        pairs = ((at["x"] - core) % 4 // 2, (y - core) % 8 // 2, (z - core) % 8 // 2, core)
        groups.setdefault(pairs, []).append((at["yl"], at["zl"], at["x"] % 2, device))
    return [[member[-1] for member in sorted(group)] for group in groups.values()]


def split_axes(core):
    return ("zh", "yh") if core == 0 else ("yh", "zh")


def split_groups(step):
    groups = {}
    for device, at in places():
        half = at["x"] // 2
        first, second = split_axes(at["core"])
        if step == 0:
            rest, place = (at["zl"], at["yl"], at[second], at["x"] % 2, at["core"]), (at[first], half)
        else:
            rest, place = (at["zl"], at["yl"], at[first], at["x"], at["core"]), (at[second],)
        groups.setdefault(rest, []).append((place, device))
    return [[device for _, device in sorted(group)] for group in groups.values()]


def owner_route():
    route = []
    for source, at in places():
        share = at["zh"] * SPLIT + at["yh"]
        x = 2 * (at["x"] % 2) + at["x"] // 2
        owner = (share // 4, share // 2 % 2, share % 2, at["yl"] * 2 + at["zl"], x, at["core"])
        route.append((source, int(np.ravel_multi_index(owner, SIZES))))
    return route


def summed_over(partial, step):
    groups = split_groups(step)
    parts = len(groups[0])
    partial = partial.reshape(parts, -1, CELLS)
    spread = lax.all_to_all(partial, AXES, split_axis=0, concat_axis=0, tiled=True, axis_index_groups=groups)
    return jnp.sum(spread.astype(jnp.float32), axis=0).astype(jnp.bfloat16)


def shards(panels, freq_weight, surface_weight, picks, neighbours):
    freq_count, parts, own_points, cells = panels.shape
    points = picks.shape[0]
    total_rows = parts * points * lax.axis_size(("zh", "zl", "yl"))
    rows = parts * own_points
    packed = pack(panels.reshape(rows, cells), freq_weight, surface_weight, picks, total_rows)
    gathered = lax.all_to_all(packed, AXES, split_axis=0, concat_axis=0, tiled=True, axis_index_groups=gather_groups())
    gathered = gathered.reshape(-1, (SET + 1) * WIDTH)
    other = blocks(gathered, False)
    arrived = lax.ppermute(other, "core", [(0, 1), (1, 0)])
    own = blocks(gathered, True)
    partial = (own.astype(jnp.float32) + arrived.astype(jnp.float32)).astype(jnp.bfloat16)
    held = summed_over(summed_over(partial, 0), 1)
    held = lax.ppermute(held, AXES, owner_route())
    return slots(held.reshape(-1, CELLS // SHARES, CELLS), neighbours)


def solution(mesh):
    fine = Mesh(mesh.devices.reshape(SIZES), AXES)
    freq, brick = ("zh", "zl", "yl"), ("yh", "x", "core")
    in_specs = (P(freq, None, brick, None), P(freq), P(), P(), P(brick, None))
    out_specs = P(brick, None, freq, None)
    return jax.shard_map(shards, mesh=fine, in_specs=in_specs, out_specs=out_specs, check_vma=False)
```

```python
import functools
import math

import jax
import jax.numpy as jnp
import numpy as np
from jax import lax
from jax.experimental import pallas as pl
from jax.experimental.pallas import tpu as pltpu
from jax.sharding import Mesh
from jax.sharding import PartitionSpec as P

CELLS = 128
BRICK_Y = 2
BRICK_Z = 3
SLAB = BRICK_Y * BRICK_Z
WIDTH = SLAB * CELLS
AXES = ("zh", "zl", "yl", "yh", "x", "core")
SIZES = (4, 2, 2, 4, 4, 2)

NEXT_PAIRS = [
    ((y * 3 + z, 6 + first), (y * 3 + z, 7 + first))
    for z, firsts in ((0, (0, 3)), (1, (0, 2, 4)), (2, (1, 4)))
    for y in range(BRICK_Y)
    for first in firsts
]
OWN_PAIRS = [
    ((0, 3), (0, 4)),
    ((1, 4), (1, 5)),
    ((2, 4), (2, 5)),
    ((0, 1), (1, 2)),
    ((1, 3), (3, 4)),
    ((4, 5), None),
]
PAIRS = NEXT_PAIRS + OWN_PAIRS
ROWS = 8 * sum(block is not None for pair in PAIRS for block in pair)
SPLIT = 4
SHARES = SPLIT * SPLIT
OWNED = 2
SET = 2 * OWNED


def block_table():
    table = np.full((SLAB, 2 * SLAB), -1, np.int32)
    for at, pair in enumerate(PAIRS):
        for half, block in enumerate(pair):
            if block is not None:
                table[block] = 2 * at + half
    return table


def pack_kernel(freq_hbm, surface_hbm, picks_hbm, panels_ref, out_ref, freq_ref, surface_ref, picks_ref, held, made, small, arrived, left, *, total_rows):
    rows, cells = held.shape
    sets = made.shape[0]
    chunks = arrived.shape[0]
    width = cells // chunks

    def fetch(chunk):
        columns = pl.ds(chunk * width, width)
        return pltpu.make_async_copy(panels_ref.at[:, columns], held.at[:, columns], arrived.at[chunk])

    def store(at):
        return pltpu.make_async_copy(made.at[at], out_ref.at[at], left.at[at])

    points = [
        pltpu.make_async_copy(surface_hbm, surface_ref, small.at[0]),
        pltpu.make_async_copy(picks_hbm, picks_ref, small.at[1]),
        pltpu.make_async_copy(freq_hbm, freq_ref, small.at[2]),
    ]
    for copy in points:
        copy.start()
    for chunk in range(chunks):
        fetch(chunk).start()
    for copy in points:
        copy.wait()
    own_points = rows // 2
    first = lax.axis_index(("yh", "x", "core")) * own_points
    row = lax.broadcasted_iota(jnp.int32, (own_points, CELLS), 0)
    picked = jnp.zeros((own_points, CELLS), jnp.float32)
    for point in range(own_points):
        picked = jnp.where(row == point, surface_ref[picks_ref[first + point]], picked)
    scale = jnp.sqrt(picked * (freq_ref[0] * (1.0 / math.sqrt(total_rows))))
    scale = jnp.concatenate([scale, scale], axis=0)
    scale = jnp.concatenate([scale] * SLAB, axis=1)
    slabs = SET * sets
    for slab in range(slabs):
        if slab * chunks % slabs == 0:
            fetch(slab * chunks // slabs).wait()
        block = (held[:, slab * WIDTH : (slab + 1) * WIDTH].astype(jnp.float32) * scale).astype(jnp.bfloat16)
        at, place = slab // SET, slab % SET
        made[at, :, place * WIDTH : (place + 1) * WIDTH] = block
        if place == 0:
            made[(at - 1) % sets, :, SET * WIDTH :] = block
            if at > 0:
                store(at - 1).start()
    store(sets - 1).start()
    for at in range(sets):
        store(at).wait()


def pack(panels, freq_weight, surface_weight, picks, total_rows):
    rows, cells = panels.shape
    sets = cells // (SET * WIDTH)
    return pl.pallas_call(
        functools.partial(pack_kernel, total_rows=total_rows),
        in_specs=[
            pl.BlockSpec(memory_space=pl.ANY),
            pl.BlockSpec(memory_space=pl.ANY),
            pl.BlockSpec(memory_space=pl.ANY),
            pl.BlockSpec(memory_space=pl.ANY),
        ],
        out_specs=pl.BlockSpec(memory_space=pl.ANY),
        out_shape=jax.ShapeDtypeStruct((sets, rows, (SET + 1) * WIDTH), jnp.bfloat16),
        scratch_shapes=[
            pltpu.SMEM(freq_weight.shape, jnp.float32),
            pltpu.SMEM(surface_weight.shape, jnp.float32),
            pltpu.SMEM(picks.shape, jnp.int32),
            pltpu.VMEM((rows, cells), jnp.bfloat16),
            pltpu.VMEM((sets, rows, (SET + 1) * WIDTH), jnp.bfloat16),
            pltpu.SemaphoreType.DMA((3,)),
            pltpu.SemaphoreType.DMA((8,)),
            pltpu.SemaphoreType.DMA((sets,)),
        ],
        compiler_params=pltpu.CompilerParams(vmem_limit_bytes=54 * 1024 * 1024),
        name="pack",
    )(freq_weight, surface_weight, picks, panels)


def blocks_kernel(gathered_ref, out_ref, turned, *, own):
    core = lax.axis_index("core")
    holder = core if own else 1 - core
    for turn in range(OWNED):
        slab_blocks(gathered_ref, out_ref, turned, holder, turn)


def slab_blocks(gathered_ref, out_ref, turned, holder, turn):
    slab = holder + OWNED * turn

    def columns(first, count):
        start = pl.multiple_of(slab * WIDTH + first * CELLS, CELLS)
        return gathered_ref[:, pl.ds(start, count * CELLS)]

    for brick in range(SLAB):
        turned[brick * CELLS : (brick + 1) * CELLS, :] = columns(brick, 1).T

    def product(bricks, first, count):
        left = jnp.concatenate([turned[b * CELLS : (b + 1) * CELLS, :] for b in bricks], axis=0)
        made = jnp.dot(left, columns(first, count), preferred_element_type=jnp.float32)
        return {
            (b, first + n): made[m * CELLS : (m + 1) * CELLS, n * CELLS : (n + 1) * CELLS]
            for m, b in enumerate(bricks)
            for n in range(count)
        }

    def store(at, pair, made):
        parts = [made[b].reshape(SHARES, CELLS // SHARES, CELLS) for b in pair if b is not None]
        rows = jnp.concatenate(parts, axis=1).astype(jnp.bfloat16)
        for share in range(SHARES):
            along_z, along_y = share // SPLIT, share % 2 * 2 + share // 2 % 2
            first = jnp.where(holder == 0, along_z, along_y)
            second = jnp.where(holder == 0, along_y, along_z)
            out_ref[first, turn, second, 16 * at : 16 * at + rows.shape[1], :] = rows[share]

    for z, firsts in ((0, (0, 3)), (1, (0, 2, 4)), (2, (1, 4))):
        bricks = (z, 3 + z)
        for first in firsts:
            made = product(bricks, SLAB + first, 2)
            for at, pair in enumerate(PAIRS):
                if pair[0] in made:
                    store(at, pair, made)
    made = product((0, 1, 2), 3, 3)
    made.update({k: v for k, v in product((0, 1), 1, 2).items() if k in ((0, 1), (1, 2))})
    made.update({k: v for k, v in product((3, 4), 4, 2).items() if k in ((3, 4), (4, 5))})
    for at in range(len(NEXT_PAIRS), len(PAIRS)):
        store(at, PAIRS[at], made)


def blocks(gathered, own):
    rows = gathered.shape[0]
    return pl.pallas_call(
        functools.partial(blocks_kernel, own=own),
        in_specs=[pl.BlockSpec(memory_space=pltpu.VMEM)],
        out_specs=pl.BlockSpec(memory_space=pltpu.VMEM),
        out_shape=jax.ShapeDtypeStruct((SPLIT, OWNED, SPLIT, ROWS, CELLS), jnp.bfloat16),
        scratch_shapes=[pltpu.VMEM((WIDTH, rows), jnp.bfloat16)],
        compiler_params=pltpu.CompilerParams(vmem_limit_bytes=16 * 1024 * 1024),
        cost_estimate=pl.CostEstimate(
            flops=OWNED * 2 * 48 * CELLS * CELLS * rows,
            bytes_accessed=OWNED * (2 * rows * 2 * WIDTH + 2 * SHARES * ROWS * CELLS),
            transcendentals=0,
        ),
        name="blocks",
    )(gathered)


def index_kernel(neighbours_ref, table_ref, index_ref):
    first = lax.axis_index(("yh", "x", "core")) * SLAB
    for b in range(index_ref.shape[0]):
        for k in range(index_ref.shape[1]):
            neighbour = neighbours_ref[b, k]
            at = table_ref[b, jnp.clip(neighbour - first, 0, 2 * SLAB - 1)]
            index_ref[b, k] = jnp.where(neighbour >= 0, at, -1)


def block_index(neighbours):
    return pl.pallas_call(
        index_kernel,
        in_specs=[pl.BlockSpec(memory_space=pltpu.SMEM)] * 2,
        out_specs=pl.BlockSpec(memory_space=pltpu.SMEM),
        out_shape=jax.ShapeDtypeStruct(neighbours.shape, jnp.int32),
        compiler_params=pltpu.CompilerParams(vmem_limit_bytes=16 * 1024 * 1024),
        name="block_index",
    )(neighbours, jnp.asarray(block_table()))


def slots_kernel(index_ref, held_ref, out_ref):
    for b in range(out_ref.shape[0]):
        for k in range(out_ref.shape[1]):
            at = index_ref[b, k]
            block = held_ref[jnp.maximum(at, 0)]
            out_ref[b, k] = jnp.where(at >= 0, block, jnp.zeros_like(block))


def slots(held, index):
    share = held.shape[1]
    return pl.pallas_call(
        slots_kernel,
        in_specs=[pl.BlockSpec(memory_space=pltpu.SMEM), pl.BlockSpec(memory_space=pltpu.VMEM)],
        out_specs=pl.BlockSpec(memory_space=pltpu.VMEM),
        out_shape=jax.ShapeDtypeStruct((*index.shape, share, CELLS), jnp.bfloat16),
        compiler_params=pltpu.CompilerParams(vmem_limit_bytes=16 * 1024 * 1024),
        name="slots",
    )(index, held)


def places():
    for device in range(math.prod(SIZES)):
        yield device, dict(zip(AXES, (int(v) for v in np.unravel_index(device, SIZES))))


def gather_groups():
    groups = {}
    for device, at in places():
        core = at["core"]
        y, z = at["yh"] * 2 + at["yl"], at["zh"] * 2 + at["zl"]
        pairs = ((at["x"] - core) % 4 // 2, (y - core) % 8 // 2, (z - core) % 8 // 2, core)
        groups.setdefault(pairs, []).append((at["yl"], at["zl"], at["x"] % 2, device))
    return [[member[-1] for member in sorted(group)] for group in groups.values()]


def split_axes(core):
    return ("zh", "yh") if core == 0 else ("yh", "zh")


def split_groups(step):
    groups = {}
    for device, at in places():
        half = at["x"] // 2
        first, second = split_axes(at["core"])
        if step == 0:
            rest, place = (at["zl"], at["yl"], at[second], at["x"] % 2, at["core"]), (at[first], half)
        else:
            rest, place = (at["zl"], at["yl"], at[first], at["x"], at["core"]), (at[second],)
        groups.setdefault(rest, []).append((place, device))
    return [[device for _, device in sorted(group)] for group in groups.values()]


def owner_route():
    route = []
    for source, at in places():
        share = at["zh"] * SPLIT + at["yh"] % 2 * 2 + at["yh"] // 2
        x = 2 * (at["x"] % 2) + at["x"] // 2
        owner = (share // 4, share // 2 % 2, share % 2, at["yl"] * 2 + at["zl"], x, at["core"])
        route.append((source, int(np.ravel_multi_index(owner, SIZES))))
    return route


def summed_over(partial, step):
    groups = split_groups(step)
    parts = len(groups[0])
    partial = partial.reshape(parts, -1, CELLS)
    spread = lax.all_to_all(partial, AXES, split_axis=0, concat_axis=0, tiled=True, axis_index_groups=groups)
    return jnp.sum(spread.astype(jnp.float32), axis=0).astype(jnp.bfloat16)


def shards(panels, freq_weight, surface_weight, picks, neighbours):
    freq_count, parts, own_points, cells = panels.shape
    points = picks.shape[0]
    total_rows = parts * points * lax.axis_size(("zh", "zl", "yl"))
    rows = parts * own_points
    packed = pack(panels.reshape(rows, cells), freq_weight, surface_weight, picks, total_rows)
    gathered = lax.all_to_all(packed, AXES, split_axis=0, concat_axis=0, tiled=True, axis_index_groups=gather_groups())
    gathered = gathered.reshape(-1, (SET + 1) * WIDTH)
    other = blocks(gathered, False)
    arrived = lax.ppermute(other, "core", [(0, 1), (1, 0)])
    own = blocks(gathered, True)
    partial = (own.astype(jnp.float32) + arrived.astype(jnp.float32)).astype(jnp.bfloat16)
    held = summed_over(summed_over(partial, 0), 1)
    neighbours, held = lax.optimization_barrier((neighbours, held))
    held = lax.ppermute(held, AXES, owner_route())
    return slots(held.reshape(-1, CELLS // SHARES, CELLS), block_index(neighbours))


def solution(mesh):
    fine = Mesh(mesh.devices.reshape(SIZES), AXES)
    freq, brick = ("zh", "zl", "yl"), ("yh", "x", "core")
    in_specs = (P(freq, None, brick, None), P(freq), P(), P(), P(brick, None))
    out_specs = P(brick, None, freq, None)
    return jax.shard_map(shards, mesh=fine, in_specs=in_specs, out_specs=out_specs, check_vma=False)
```

```python
import functools
import math

import jax
import jax.numpy as jnp
import numpy as np
from jax import lax
from jax.experimental import pallas as pl
from jax.experimental.pallas import tpu as pltpu
from jax.sharding import Mesh
from jax.sharding import PartitionSpec as P

CELLS = 128
BRICK_Y = 2
BRICK_Z = 3
SLAB = BRICK_Y * BRICK_Z
WIDTH = SLAB * CELLS
AXES = ("zh", "zl", "yl", "yh", "x", "core")
SIZES = (4, 2, 2, 4, 4, 2)

NEXT_PAIRS = [
    ((y * 3 + z, 6 + first), (y * 3 + z, 7 + first))
    for z, firsts in ((0, (0, 3)), (1, (0, 2, 4)), (2, (1, 4)))
    for y in range(BRICK_Y)
    for first in firsts
]
OWN_PAIRS = [
    ((0, 3), (0, 4)),
    ((1, 4), (1, 5)),
    ((2, 4), (2, 5)),
    ((0, 1), (1, 2)),
    ((1, 3), (3, 4)),
    ((4, 5), None),
]
PAIRS = NEXT_PAIRS + OWN_PAIRS
ROWS = 8 * sum(block is not None for pair in PAIRS for block in pair)
SPLIT = 4
SHARES = SPLIT * SPLIT
OWNED = 2
SET = 2 * OWNED


def block_table():
    table = np.full((SLAB, 2 * SLAB), -1, np.int32)
    for at, pair in enumerate(PAIRS):
        for half, block in enumerate(pair):
            if block is not None:
                table[block] = 2 * at + half
    return table


def pack_kernel(freq_hbm, surface_hbm, picks_hbm, panels_ref, out_ref, freq_ref, surface_ref, picks_ref, held, made, small, arrived, left, *, total_rows):
    rows, cells = held.shape
    sets = made.shape[0]
    chunks = arrived.shape[0]
    width = cells // chunks

    def fetch(chunk):
        columns = pl.ds(chunk * width, width)
        return pltpu.make_async_copy(panels_ref.at[:, columns], held.at[:, columns], arrived.at[chunk])

    def store(at):
        return pltpu.make_async_copy(made.at[at], out_ref.at[at], left.at[at])

    points = [
        pltpu.make_async_copy(surface_hbm, surface_ref, small.at[0]),
        pltpu.make_async_copy(picks_hbm, picks_ref, small.at[1]),
        pltpu.make_async_copy(freq_hbm, freq_ref, small.at[2]),
    ]
    for copy in points:
        copy.start()
    for chunk in range(chunks):
        fetch(chunk).start()
    for copy in points:
        copy.wait()
    own_points = rows // 2
    first = lax.axis_index(("yh", "x", "core")) * own_points
    row = lax.broadcasted_iota(jnp.int32, (own_points, CELLS), 0)
    picked = jnp.zeros((own_points, CELLS), jnp.float32)
    for point in range(own_points):
        picked = jnp.where(row == point, surface_ref[picks_ref[first + point]], picked)
    scale = jnp.sqrt(picked * (freq_ref[0] * (1.0 / math.sqrt(total_rows))))
    scale = jnp.concatenate([scale, scale], axis=0)
    scale = jnp.concatenate([scale] * SLAB, axis=1)
    slabs = SET * sets
    for slab in range(slabs):
        if slab * chunks % slabs == 0:
            fetch(slab * chunks // slabs).wait()
        block = (held[:, slab * WIDTH : (slab + 1) * WIDTH].astype(jnp.float32) * scale).astype(jnp.bfloat16)
        at, place = slab // SET, slab % SET
        made[at, :, place * WIDTH : (place + 1) * WIDTH] = block
        if place == 0:
            made[(at - 1) % sets, :, SET * WIDTH :] = block
            if at > 0:
                store(at - 1).start()
    store(sets - 1).start()
    for at in range(sets):
        store(at).wait()


def pack(panels, freq_weight, surface_weight, picks, total_rows):
    rows, cells = panels.shape
    sets = cells // (SET * WIDTH)
    return pl.pallas_call(
        functools.partial(pack_kernel, total_rows=total_rows),
        in_specs=[
            pl.BlockSpec(memory_space=pl.ANY),
            pl.BlockSpec(memory_space=pl.ANY),
            pl.BlockSpec(memory_space=pl.ANY),
            pl.BlockSpec(memory_space=pl.ANY),
        ],
        out_specs=pl.BlockSpec(memory_space=pl.ANY),
        out_shape=jax.ShapeDtypeStruct((sets, rows, (SET + 1) * WIDTH), jnp.bfloat16),
        scratch_shapes=[
            pltpu.SMEM(freq_weight.shape, jnp.float32),
            pltpu.SMEM(surface_weight.shape, jnp.float32),
            pltpu.SMEM(picks.shape, jnp.int32),
            pltpu.VMEM((rows, cells), jnp.bfloat16),
            pltpu.VMEM((sets, rows, (SET + 1) * WIDTH), jnp.bfloat16),
            pltpu.SemaphoreType.DMA((3,)),
            pltpu.SemaphoreType.DMA((8,)),
            pltpu.SemaphoreType.DMA((sets,)),
        ],
        compiler_params=pltpu.CompilerParams(vmem_limit_bytes=54 * 1024 * 1024),
        name="pack",
    )(freq_weight, surface_weight, picks, panels)


def blocks_kernel(gathered_ref, out_ref, turned, *, own):
    core = lax.axis_index("core")
    holder = core if own else 1 - core
    for turn in range(OWNED):
        slab_blocks(gathered_ref, out_ref, turned, holder, turn)


def slab_blocks(gathered_ref, out_ref, turned, holder, turn):
    slab = holder + OWNED * turn

    def columns(first, count):
        start = pl.multiple_of(slab * WIDTH + first * CELLS, CELLS)
        return gathered_ref[:, pl.ds(start, count * CELLS)]

    for brick in range(SLAB):
        turned[brick * CELLS : (brick + 1) * CELLS, :] = columns(brick, 1).T

    def product(bricks, first, count):
        left = jnp.concatenate([turned[b * CELLS : (b + 1) * CELLS, :] for b in bricks], axis=0)
        made = jnp.dot(left, columns(first, count), preferred_element_type=jnp.float32)
        return {
            (b, first + n): made[m * CELLS : (m + 1) * CELLS, n * CELLS : (n + 1) * CELLS]
            for m, b in enumerate(bricks)
            for n in range(count)
        }

    def store(at, pair, made):
        parts = [made[b].reshape(SHARES, CELLS // SHARES, CELLS) for b in pair if b is not None]
        rows = jnp.concatenate(parts, axis=1).astype(jnp.bfloat16)
        for share in range(SHARES):
            along_z, along_y = share // SPLIT, share % 2 * 2 + share // 2 % 2
            first = jnp.where(holder == 0, along_z, along_y)
            second = jnp.where(holder == 0, along_y, along_z)
            out_ref[first, turn, second, 16 * at : 16 * at + rows.shape[1], :] = rows[share]

    for z, firsts in ((0, (0, 3)), (1, (0, 2, 4)), (2, (1, 4))):
        bricks = (z, 3 + z)
        for first in firsts:
            made = product(bricks, SLAB + first, 2)
            for at, pair in enumerate(PAIRS):
                if pair[0] in made:
                    store(at, pair, made)
    made = {}
    for bricks, first in (((0, 1), 3), ((1, 2), 4), ((0, 1), 1), ((3, 4), 4)):
        made.update({block: value for block, value in product(bricks, first, 2).items() if block not in made})
    for at in range(len(NEXT_PAIRS), len(PAIRS)):
        store(at, PAIRS[at], made)


def blocks(gathered, own):
    rows = gathered.shape[0]
    return pl.pallas_call(
        functools.partial(blocks_kernel, own=own),
        in_specs=[pl.BlockSpec(memory_space=pltpu.VMEM)],
        out_specs=pl.BlockSpec(memory_space=pltpu.VMEM),
        out_shape=jax.ShapeDtypeStruct((SPLIT, OWNED, SPLIT, ROWS, CELLS), jnp.bfloat16),
        scratch_shapes=[pltpu.VMEM((WIDTH, rows), jnp.bfloat16)],
        compiler_params=pltpu.CompilerParams(vmem_limit_bytes=16 * 1024 * 1024),
        cost_estimate=pl.CostEstimate(
            flops=OWNED * 2 * 44 * CELLS * CELLS * rows,
            bytes_accessed=OWNED * (2 * rows * 2 * WIDTH + 2 * SHARES * ROWS * CELLS),
            transcendentals=0,
        ),
        name="blocks",
    )(gathered)


def index_kernel(neighbours_ref, table_ref, index_ref):
    first = lax.axis_index(("yh", "x", "core")) * SLAB
    for b in range(index_ref.shape[0]):
        for k in range(index_ref.shape[1]):
            neighbour = neighbours_ref[b, k]
            at = table_ref[b, jnp.clip(neighbour - first, 0, 2 * SLAB - 1)]
            index_ref[b, k] = jnp.where(neighbour >= 0, at, -1)


def block_index(neighbours):
    return pl.pallas_call(
        index_kernel,
        in_specs=[pl.BlockSpec(memory_space=pltpu.SMEM)] * 2,
        out_specs=pl.BlockSpec(memory_space=pltpu.SMEM),
        out_shape=jax.ShapeDtypeStruct(neighbours.shape, jnp.int32),
        compiler_params=pltpu.CompilerParams(vmem_limit_bytes=16 * 1024 * 1024),
        name="block_index",
    )(neighbours, jnp.asarray(block_table()))


def slots_kernel(index_ref, held_ref, out_ref):
    for b in range(out_ref.shape[0]):
        for k in range(out_ref.shape[1]):
            at = index_ref[b, k]
            block = held_ref[jnp.maximum(at, 0)]
            out_ref[b, k] = jnp.where(at >= 0, block, jnp.zeros_like(block))


def slots(held, index):
    share = held.shape[1]
    return pl.pallas_call(
        slots_kernel,
        in_specs=[pl.BlockSpec(memory_space=pltpu.SMEM), pl.BlockSpec(memory_space=pltpu.VMEM)],
        out_specs=pl.BlockSpec(memory_space=pltpu.VMEM),
        out_shape=jax.ShapeDtypeStruct((*index.shape, share, CELLS), jnp.bfloat16),
        compiler_params=pltpu.CompilerParams(vmem_limit_bytes=16 * 1024 * 1024),
        name="slots",
    )(index, held)


def places():
    for device in range(math.prod(SIZES)):
        yield device, dict(zip(AXES, (int(v) for v in np.unravel_index(device, SIZES))))


def gather_groups():
    groups = {}
    for device, at in places():
        core = at["core"]
        y, z = at["yh"] * 2 + at["yl"], at["zh"] * 2 + at["zl"]
        pairs = ((at["x"] - core) % 4 // 2, (y - core) % 8 // 2, (z - core) % 8 // 2, core)
        groups.setdefault(pairs, []).append((at["yl"], at["zl"], at["x"] % 2, device))
    return [[member[-1] for member in sorted(group)] for group in groups.values()]


def split_axes(core):
    return ("zh", "yh") if core == 0 else ("yh", "zh")


def split_groups(step):
    groups = {}
    for device, at in places():
        half = at["x"] // 2
        first, second = split_axes(at["core"])
        if step == 0:
            rest, place = (at["zl"], at["yl"], at[second], at["x"] % 2, at["core"]), (at[first], half)
        else:
            rest, place = (at["zl"], at["yl"], at[first], at["x"], at["core"]), (at[second],)
        groups.setdefault(rest, []).append((place, device))
    return [[device for _, device in sorted(group)] for group in groups.values()]


def owner_route():
    route = []
    for source, at in places():
        share = at["zh"] * SPLIT + at["yh"] % 2 * 2 + at["yh"] // 2
        x = 2 * (at["x"] % 2) + at["x"] // 2
        owner = (share // 4, share // 2 % 2, share % 2, at["yl"] * 2 + at["zl"], x, at["core"])
        route.append((source, int(np.ravel_multi_index(owner, SIZES))))
    return route


def summed_over(partial, step):
    groups = split_groups(step)
    parts = len(groups[0])
    partial = partial.reshape(parts, -1, CELLS)
    spread = lax.all_to_all(partial, AXES, split_axis=0, concat_axis=0, tiled=True, axis_index_groups=groups)
    return jnp.sum(spread.astype(jnp.float32), axis=0).astype(jnp.bfloat16)


def shards(panels, freq_weight, surface_weight, picks, neighbours):
    freq_count, parts, own_points, cells = panels.shape
    points = picks.shape[0]
    total_rows = parts * points * lax.axis_size(("zh", "zl", "yl"))
    rows = parts * own_points
    packed = pack(panels.reshape(rows, cells), freq_weight, surface_weight, picks, total_rows)
    gathered = lax.all_to_all(packed, AXES, split_axis=0, concat_axis=0, tiled=True, axis_index_groups=gather_groups())
    gathered = gathered.reshape(-1, (SET + 1) * WIDTH)
    other = blocks(gathered, False)
    arrived = lax.ppermute(other, "core", [(0, 1), (1, 0)])
    own = blocks(gathered, True)
    partial = (own.astype(jnp.float32) + arrived.astype(jnp.float32)).astype(jnp.bfloat16)
    held = summed_over(summed_over(partial, 0), 1)
    neighbours, held = lax.optimization_barrier((neighbours, held))
    held = lax.ppermute(held, AXES, owner_route())
    return slots(held.reshape(-1, CELLS // SHARES, CELLS), block_index(neighbours))


def solution(mesh):
    fine = Mesh(mesh.devices.reshape(SIZES), AXES)
    freq, brick = ("zh", "zl", "yl"), ("yh", "x", "core")
    in_specs = (P(freq, None, brick, None), P(freq), P(), P(), P(brick, None))
    out_specs = P(brick, None, freq, None)
    return jax.shard_map(shards, mesh=fine, in_specs=in_specs, out_specs=out_specs, check_vma=False)
```

```python
import functools
import math

import jax
import jax.numpy as jnp
import numpy as np
from jax import lax
from jax.experimental import pallas as pl
from jax.experimental.pallas import tpu as pltpu
from jax.sharding import Mesh
from jax.sharding import PartitionSpec as P

CELLS = 128
BRICK_Y = 2
BRICK_Z = 3
SLAB = BRICK_Y * BRICK_Z
WIDTH = SLAB * CELLS
AXES = ("zh", "zl", "yl", "yh", "x", "core")
SIZES = (4, 2, 2, 4, 4, 2)

NEXT_PAIRS = [
    ((y * 3 + z, 6 + first), (y * 3 + z, 7 + first))
    for z, firsts in ((0, (0, 3)), (1, (0, 2, 4)), (2, (1, 4)))
    for y in range(BRICK_Y)
    for first in firsts
]
OWN_PAIRS = [
    ((0, 3), (0, 4)),
    ((1, 4), (1, 5)),
    ((2, 4), (2, 5)),
    ((0, 1), (1, 2)),
    ((1, 3), (3, 4)),
    ((4, 5), None),
]
PAIRS = NEXT_PAIRS + OWN_PAIRS
ROWS = 8 * sum(block is not None for pair in PAIRS for block in pair)
SPLIT = 4
SHARES = SPLIT * SPLIT
OWNED = 2
SET = 2 * OWNED


def block_table():
    table = np.full((SLAB, 2 * SLAB), -1, np.int32)
    for at, pair in enumerate(PAIRS):
        for half, block in enumerate(pair):
            if block is not None:
                table[block] = 2 * at + half
    return table


def pack_kernel(freq_hbm, surface_hbm, picks_hbm, panels_ref, out_ref, freq_ref, surface_ref, picks_ref, held, made, small, arrived, left, *, total_rows):
    rows, cells = held.shape
    sets = made.shape[0]
    chunks = arrived.shape[0]
    width = cells // chunks

    def fetch(chunk):
        columns = pl.ds(chunk * width, width)
        return pltpu.make_async_copy(panels_ref.at[:, columns], held.at[:, columns], arrived.at[chunk])

    def store(at, part):
        columns = pl.ds(0, OWNED * WIDTH) if part == 0 else pl.ds(OWNED * WIDTH, (SET + 1 - OWNED) * WIDTH)
        return pltpu.make_async_copy(made.at[at, :, columns], out_ref.at[at, :, columns], left.at[at, part])

    points = [
        pltpu.make_async_copy(surface_hbm, surface_ref, small.at[0]),
        pltpu.make_async_copy(picks_hbm, picks_ref, small.at[1]),
        pltpu.make_async_copy(freq_hbm, freq_ref, small.at[2]),
    ]
    for copy in points:
        copy.start()
    for chunk in range(chunks):
        fetch(chunk).start()
    for copy in points:
        copy.wait()
    own_points = rows // 2
    first = lax.axis_index(("yh", "x", "core")) * own_points
    row = lax.broadcasted_iota(jnp.int32, (own_points, CELLS), 0)
    picked = jnp.zeros((own_points, CELLS), jnp.float32)
    for point in range(own_points):
        picked = jnp.where(row == point, surface_ref[picks_ref[first + point]], picked)
    scale = jnp.sqrt(picked * (freq_ref[0] * (1.0 / math.sqrt(total_rows))))
    scale = jnp.concatenate([scale, scale], axis=0)
    scale = jnp.concatenate([scale] * SLAB, axis=1)
    slabs = SET * sets
    for slab in range(slabs):
        if slab * chunks % slabs == 0:
            fetch(slab * chunks // slabs).wait()
        block = (held[:, slab * WIDTH : (slab + 1) * WIDTH].astype(jnp.float32) * scale).astype(jnp.bfloat16)
        at, place = slab // SET, slab % SET
        made[at, :, place * WIDTH : (place + 1) * WIDTH] = block
        if place == 0:
            made[(at - 1) % sets, :, SET * WIDTH :] = block
            if at > 0:
                store(at - 1, 1).start()
        elif place == OWNED - 1:
            store(at, 0).start()
    store(sets - 1, 1).start()
    for at in range(sets):
        store(at, 0).wait()
        store(at, 1).wait()


def pack(panels, freq_weight, surface_weight, picks, total_rows):
    rows, cells = panels.shape
    sets = cells // (SET * WIDTH)
    return pl.pallas_call(
        functools.partial(pack_kernel, total_rows=total_rows),
        in_specs=[
            pl.BlockSpec(memory_space=pl.ANY),
            pl.BlockSpec(memory_space=pl.ANY),
            pl.BlockSpec(memory_space=pl.ANY),
            pl.BlockSpec(memory_space=pl.ANY),
        ],
        out_specs=pl.BlockSpec(memory_space=pl.ANY),
        out_shape=jax.ShapeDtypeStruct((sets, rows, (SET + 1) * WIDTH), jnp.bfloat16),
        scratch_shapes=[
            pltpu.SMEM(freq_weight.shape, jnp.float32),
            pltpu.SMEM(surface_weight.shape, jnp.float32),
            pltpu.SMEM(picks.shape, jnp.int32),
            pltpu.VMEM((rows, cells), jnp.bfloat16),
            pltpu.VMEM((sets, rows, (SET + 1) * WIDTH), jnp.bfloat16),
            pltpu.SemaphoreType.DMA((3,)),
            pltpu.SemaphoreType.DMA((16,)),
            pltpu.SemaphoreType.DMA((sets, 2)),
        ],
        compiler_params=pltpu.CompilerParams(vmem_limit_bytes=54 * 1024 * 1024),
        name="pack",
    )(freq_weight, surface_weight, picks, panels)


def blocks_kernel(gathered_ref, out_ref, turned, *, own):
    core = lax.axis_index("core")
    holder = core if own else 1 - core
    for turn in range(OWNED):
        slab_blocks(gathered_ref, out_ref, turned, holder, turn)


def slab_blocks(gathered_ref, out_ref, turned, holder, turn):
    slab = holder + OWNED * turn

    def columns(first, count):
        start = pl.multiple_of(slab * WIDTH + first * CELLS, CELLS)
        return gathered_ref[:, pl.ds(start, count * CELLS)]

    for brick in range(SLAB):
        turned[brick * CELLS : (brick + 1) * CELLS, :] = columns(brick, 1).T

    def product(bricks, first, count):
        left = jnp.concatenate([turned[b * CELLS : (b + 1) * CELLS, :] for b in bricks], axis=0)
        made = jnp.dot(left, columns(first, count), preferred_element_type=jnp.float32)
        return {
            (b, first + n): made[m * CELLS : (m + 1) * CELLS, n * CELLS : (n + 1) * CELLS]
            for m, b in enumerate(bricks)
            for n in range(count)
        }

    def store(at, pair, made):
        parts = [made[b].reshape(SHARES, CELLS // SHARES, CELLS) for b in pair if b is not None]
        rows = jnp.concatenate(parts, axis=1).astype(jnp.bfloat16)
        for share in range(SHARES):
            along_z, along_y = share // SPLIT, share % 2 * 2 + share // 2 % 2
            first = jnp.where(holder == 0, along_z, along_y)
            second = jnp.where(holder == 0, along_y, along_z)
            out_ref[first, turn, second, 16 * at : 16 * at + rows.shape[1], :] = rows[share]

    for z, firsts in ((0, (0, 3)), (1, (0, 2, 4)), (2, (1, 4))):
        bricks = (z, 3 + z)
        for first in firsts:
            made = product(bricks, SLAB + first, 2)
            for at, pair in enumerate(PAIRS):
                if pair[0] in made:
                    store(at, pair, made)
    made = {}
    for bricks, first in (((0, 1), 3), ((1, 2), 4), ((0, 1), 1), ((3, 4), 4)):
        made.update({block: value for block, value in product(bricks, first, 2).items() if block not in made})
    for at in range(len(NEXT_PAIRS), len(PAIRS)):
        store(at, PAIRS[at], made)


def blocks(gathered, own):
    rows = gathered.shape[0]
    return pl.pallas_call(
        functools.partial(blocks_kernel, own=own),
        in_specs=[pl.BlockSpec(memory_space=pltpu.VMEM)],
        out_specs=pl.BlockSpec(memory_space=pltpu.VMEM),
        out_shape=jax.ShapeDtypeStruct((SPLIT, OWNED, SPLIT, ROWS, CELLS), jnp.bfloat16),
        scratch_shapes=[pltpu.VMEM((WIDTH, rows), jnp.bfloat16)],
        compiler_params=pltpu.CompilerParams(vmem_limit_bytes=16 * 1024 * 1024),
        cost_estimate=pl.CostEstimate(
            flops=OWNED * 2 * 44 * CELLS * CELLS * rows,
            bytes_accessed=OWNED * (2 * rows * 2 * WIDTH + 2 * SHARES * ROWS * CELLS),
            transcendentals=0,
        ),
        name="blocks",
    )(gathered)


def index_kernel(neighbours_ref, table_ref, index_ref):
    first = lax.axis_index(("yh", "x", "core")) * SLAB
    for b in range(index_ref.shape[0]):
        for k in range(index_ref.shape[1]):
            neighbour = neighbours_ref[b, k]
            at = table_ref[b, jnp.clip(neighbour - first, 0, 2 * SLAB - 1)]
            index_ref[b, k] = jnp.where(neighbour >= 0, at, -1)


def block_index(neighbours):
    return pl.pallas_call(
        index_kernel,
        in_specs=[pl.BlockSpec(memory_space=pltpu.SMEM)] * 2,
        out_specs=pl.BlockSpec(memory_space=pltpu.SMEM),
        out_shape=jax.ShapeDtypeStruct(neighbours.shape, jnp.int32),
        compiler_params=pltpu.CompilerParams(vmem_limit_bytes=16 * 1024 * 1024),
        name="block_index",
    )(neighbours, jnp.asarray(block_table()))


def slots_kernel(index_ref, held_ref, out_ref):
    for b in range(out_ref.shape[0]):
        for k in range(out_ref.shape[1]):
            at = index_ref[b, k]
            block = held_ref[jnp.maximum(at, 0)]
            out_ref[b, k] = jnp.where(at >= 0, block, jnp.zeros_like(block))


def slots(held, index):
    share = held.shape[1]
    return pl.pallas_call(
        slots_kernel,
        in_specs=[pl.BlockSpec(memory_space=pltpu.SMEM), pl.BlockSpec(memory_space=pltpu.VMEM)],
        out_specs=pl.BlockSpec(memory_space=pltpu.VMEM),
        out_shape=jax.ShapeDtypeStruct((*index.shape, share, CELLS), jnp.bfloat16),
        compiler_params=pltpu.CompilerParams(vmem_limit_bytes=16 * 1024 * 1024),
        name="slots",
    )(index, held)


def places():
    for device in range(math.prod(SIZES)):
        yield device, dict(zip(AXES, (int(v) for v in np.unravel_index(device, SIZES))))


def gather_groups():
    groups = {}
    for device, at in places():
        core = at["core"]
        y, z = at["yh"] * 2 + at["yl"], at["zh"] * 2 + at["zl"]
        pairs = ((at["x"] - core) % 4 // 2, (y - core) % 8 // 2, (z - core) % 8 // 2, core)
        groups.setdefault(pairs, []).append((at["yl"], at["zl"], at["x"] % 2, device))
    return [[member[-1] for member in sorted(group)] for group in groups.values()]


def split_axes(core):
    return ("zh", "yh") if core == 0 else ("yh", "zh")


def split_groups(step):
    groups = {}
    for device, at in places():
        half = at["x"] // 2
        first, second = split_axes(at["core"])
        if step == 0:
            rest, place = (at["zl"], at["yl"], at[second], at["x"] % 2, at["core"]), (at[first], half)
        else:
            rest, place = (at["zl"], at["yl"], at[first], at["x"], at["core"]), (at[second],)
        groups.setdefault(rest, []).append((place, device))
    return [[device for _, device in sorted(group)] for group in groups.values()]


def owner_route():
    route = []
    for source, at in places():
        share = at["zh"] * SPLIT + at["yh"] % 2 * 2 + at["yh"] // 2
        x = 2 * (at["x"] % 2) + at["x"] // 2
        owner = (share // 4, share // 2 % 2, share % 2, at["yl"] * 2 + at["zl"], x, at["core"])
        route.append((source, int(np.ravel_multi_index(owner, SIZES))))
    return route


def summed_over(partial, step):
    groups = split_groups(step)
    parts = len(groups[0])
    partial = partial.reshape(parts, -1, CELLS)
    spread = lax.all_to_all(partial, AXES, split_axis=0, concat_axis=0, tiled=True, axis_index_groups=groups)
    return jnp.sum(spread.astype(jnp.float32), axis=0).astype(jnp.bfloat16)


def shards(panels, freq_weight, surface_weight, picks, neighbours):
    freq_count, parts, own_points, cells = panels.shape
    points = picks.shape[0]
    total_rows = parts * points * lax.axis_size(("zh", "zl", "yl"))
    rows = parts * own_points
    packed = pack(panels.reshape(rows, cells), freq_weight, surface_weight, picks, total_rows)
    gathered = lax.all_to_all(packed, AXES, split_axis=0, concat_axis=0, tiled=True, axis_index_groups=gather_groups())
    gathered = gathered.reshape(-1, (SET + 1) * WIDTH)
    other = blocks(gathered, False)
    arrived = lax.ppermute(other, "core", [(0, 1), (1, 0)])
    own = blocks(gathered, True)
    partial = (own.astype(jnp.float32) + arrived.astype(jnp.float32)).astype(jnp.bfloat16)
    held = summed_over(summed_over(partial, 0), 1)
    neighbours, held = lax.optimization_barrier((neighbours, held))
    held = lax.ppermute(held, AXES, owner_route())
    return slots(held.reshape(-1, CELLS // SHARES, CELLS), block_index(neighbours))


def solution(mesh):
    fine = Mesh(mesh.devices.reshape(SIZES), AXES)
    freq, brick = ("zh", "zl", "yl"), ("yh", "x", "core")
    in_specs = (P(freq, None, brick, None), P(freq), P(), P(), P(brick, None))
    out_specs = P(brick, None, freq, None)
    return jax.shard_map(shards, mesh=fine, in_specs=in_specs, out_specs=out_specs, check_vma=False)
```
